128 devices in a mesh: depth: 4 (over x), row: 16 (over z, y), col: 2 (over core).
Axes of the slice: x: 4, y: 4, z: 4, core: 2. Of those that a mesh axis runs over, the one named last changes fastest.
Arguments:
- acts: bfloat16 [1024, 6144], P(('depth', 'col'), 'row'), may hold values from -6 to 6
- cotangent: bfloat16 [1024, 6144], P(('depth', 'col'), 'row'), may hold values from -6 to 6
- pre_act: bfloat16 [1024, 12288], P(('depth', 'row'), 'col'), may hold values from -8 to 8
- w_in: bfloat16 [6144, 12288], P('row', 'col'), may hold values from -0.078125 to 0.078125
- w_out: bfloat16 [12288, 6144], P('col', 'row'), may hold values from -0.0546875 to 0.0546875
Outputs:
- grad_in: float32 [1024, 6144], P(('depth', 'col'), 'row')
- grad_w_in: float32 [16, 4, 96, 12288], P('row', 'depth', None, 'col')
- grad_w_out: float32 [2, 4, 1536, 6144], P('col', 'depth', None, 'row')
The draws below stay inside these ranges and needn't reach their ends.
All inputs are finite; a program needn't handle non-finite values.
Results may differ from the reference program's by a relative error of at most 0.0029.
Values may be sent and summed in bfloat16 or wider, within the bound.
A program may use at most 128 MiB of HBM per device.

```python
import math
import jax
import jax.numpy as jnp
from jax import lax

D = 6144
FFW = 12288
SLICE_TOK = 256
TOKENS = 1024
N_DEPTH = 4
N_ROW = 16
N_COL = 2


def block_scale(key, extent, shards, smallest, top_value):
    gain = 1.0
    for axis_at, blocks in shards:
        steps = jax.random.uniform(jax.random.fold_in(jax.random.fold_in(key, 6), axis_at), (blocks,), jnp.float32, smallest / len(shards), top_value / len(shards))
        gain = gain * jnp.repeat(jnp.exp(steps), extent[axis_at] // blocks).reshape((-1,) + (1,) * (len(extent) - 1 - axis_at))
    return gain


def centred(own_key, dims, deviation, most, pieces=(), held_as=jnp.bfloat16):
    array = deviation * jax.random.normal(own_key, dims, jnp.float32)
    if pieces:
        array = array * block_scale(own_key, dims, pieces, -0.22, 0.18)
    return jnp.clip(array, -most, most).astype(held_as)


def setup_inputs(seed: int = 0) -> dict:
    key_list = jax.random.split(jax.random.key(seed), 6)
    return {
        "acts": centred(key_list[0], (TOKENS, D), 1.0, 6.0, ((0, 8), (1, 16))),
        "cotangent": centred(key_list[1], (TOKENS, D), 1.0, 6.0, ((0, 8), (1, 16))),
        "pre_act": centred(key_list[2], (TOKENS, FFW), 1.5, 8.0, ((0, 64), (1, 2))),
        "w_in": centred(key_list[3], (D, FFW), D ** -0.5, 0.078125, ((0, 16), (1, 2))),
        "w_out": centred(key_list[4], (FFW, D), FFW ** -0.5, 0.0546875, ((0, 2), (1, 16))),
    }


gelu_coef = 0.044715

def gelu_value(v):
    inner = math.sqrt(2.0 / math.pi) * (v + gelu_coef * v * v * v)
    return 0.5 * v * (1.0 + jnp.tanh(inner))

def gelu_slope(v):
    inner = math.sqrt(2.0 / math.pi) * (v + gelu_coef * v * v * v)
    tanh_u = jnp.tanh(inner)
    return 0.5 * (1.0 + tanh_u) + 0.5 * v * (1.0 - tanh_u * tanh_u) * math.sqrt(2.0 / math.pi) * (1.0 + 3.0 * gelu_coef * v * v)

def reference(acts, cotangent, pre_act, w_in, w_out):
    pre = pre_act.astype(jnp.float32)
    grad_act = lax.dot_general(cotangent, w_out, (((1,), (1,)), ((), ())), preferred_element_type=jnp.float32)
    grad_pre = (grad_act * gelu_slope(pre)).astype(jnp.bfloat16)
    hidden = gelu_value(pre).astype(jnp.bfloat16)
    grad_in = lax.dot_general(grad_pre, w_in, (((1,), (1,)), ((), ())), preferred_element_type=jnp.float32)
    norm_factor = 1.0 / math.sqrt(TOKENS)

    def one_slice(carry, index):
        start = (index * SLICE_TOK).astype(jnp.int32)
        acts_s = lax.dynamic_slice_in_dim(acts, start, SLICE_TOK, 0)
        cot_s = lax.dynamic_slice_in_dim(cotangent, start, SLICE_TOK, 0)
        pre_s = lax.dynamic_slice_in_dim(grad_pre, start, SLICE_TOK, 0)
        hid_s = lax.dynamic_slice_in_dim(hidden, start, SLICE_TOK, 0)
        part_in = lax.dot_general(acts_s, pre_s, (((0,), (0,)), ((), ())), preferred_element_type=jnp.float32) * norm_factor
        part_out = lax.dot_general(hid_s, cot_s, (((0,), (0,)), ((), ())), preferred_element_type=jnp.float32) * norm_factor
        return ((carry[0] + part_in, carry[1] + part_out), None)
    start_sums = (jnp.zeros((D, FFW), jnp.float32), jnp.zeros((FFW, D), jnp.float32))
    sums, unused = lax.scan(one_slice, start_sums, jnp.arange(N_DEPTH, dtype=jnp.int32))
    grad_w_in = sums[0].reshape(N_ROW, N_DEPTH, D // (N_ROW * N_DEPTH), FFW)
    grad_w_out = sums[1].reshape(N_COL, N_DEPTH, FFW // (N_COL * N_DEPTH), D)
    return (grad_in, grad_w_in, grad_w_out)
```

```python
import functools
import math

import jax
import jax.numpy as jnp
from jax import lax
from jax.experimental import pallas as pl
from jax.experimental.pallas import tpu as pltpu
from jax.sharding import PartitionSpec as P

MESH = pl.DeviceIdType.MESH
F32, BF16 = jnp.float32, jnp.bfloat16
RING = 4
WIDTHS = (1024, 1024, 1024, 1024, 1024, 1024)
ORDER = (
    2, 2, 3, 3, 4, 4, 5, 5, 8, 2, 0, 3, 0, 8, 5, 4, 2, 1, 3, 1, 5, 0, 4, 7, 1, 6, 3, 2, 5, 0, 1, 4,
    6, 3, 2, 5, 7, 0, 4, 1, 3, 2, 0, 5, 1, 8, 2, 4, 3, 0, 5, 2, 1, 4, 3, 3, 0, 5, 1, 6, 7, 5, 0, 2,
    1, 4, 1, 0, 4, 6, 7, 3, 9, 4, 1, 2, 0, 6, 5, 6, 7, 7, 9,
)
TILE = 768

gelu_coef = 0.044715
root = math.sqrt(2.0 / math.pi)


def gelu_and_slope(v):
    tanh_u = jnp.tanh(root * (v + gelu_coef * v * v * v))
    gelu = 0.5 * v * (1.0 + tanh_u)
    slope = 0.5 * (1.0 + tanh_u) + 0.5 * v * (1.0 - tanh_u * tanh_u) * root * (
        1.0 + 3.0 * gelu_coef * v * v
    )
    return gelu, slope


def nt(left, right):
    return lax.dot_general(
        left, right, (((1,), (1,)), ((), ())), preferred_element_type=F32
    )


def nn(left, right):
    return lax.dot_general(
        left, right, (((1,), (0,)), ((), ())), preferred_element_type=F32
    )


SHIFT = 2.0**20


def coded(v):
    v = v * jnp.abs(v)
    return (v * jnp.abs(v)).astype(BF16)


def decoded(t):
    t = t.astype(F32)
    r = lax.rsqrt(jnp.maximum(jnp.abs(t), 1e-37))
    return (t * r) * (r * lax.rsqrt(r))


def tn(left, right):
    return lax.dot_general(
        left, right, (((0,), (0,)), ((), ())), preferred_element_type=F32
    )


class Copies:
    def __init__(self, send_sems, recv_sems):
        self.send_sems, self.recv_sems = send_sems, recv_sems
        self.all, self.settled = [], 0

    def send(self, src, dst, to):
        n = len(self.all)
        copy = pltpu.make_async_remote_copy(
            src_ref=src,
            dst_ref=dst,
            send_sem=self.send_sems.at[n],
            recv_sem=self.recv_sems.at[n],
            device_id=to,
            device_id_type=MESH,
        )
        copy.start()
        self.all.append(copy)
        return copy


def kernel(
    n_copies, norm_factor, acts, cot, pre, w_in, w_out,
    gi_out, gwi_out, gwo_out,
    hid_full, acts_in, pre_v, w_in_v, w_out_v, cot_v, cot_scaled, cot_full, gwi_recv, gi, gi_recv, gi_sum, gi_depth,
    acts_v, acts_x, acts_all, slope_v, hid_v,
    part, part16, relay1, final1, mid, mid16, final2, gp, gq, xpart,
    send_sems, recv_sems, local_sems,
):
    x, row, c = lax.axis_index("depth"), lax.axis_index("row"), lax.axis_index("col")
    z, y = row // RING, row % RING
    feats, hid_size = w_in.shape
    toks, rows = acts.shape[0], feats // RING
    starts = [sum(WIDTHS[:k]) for k in range(len(WIDTHS))]

    def turn(i, step):
        return lax.rem(i + (step + RING), RING)

    def at(axis, step):
        if axis == "x":
            return (turn(x, step), row, c)
        if axis == "z":
            return (x, turn(z, step) * RING + y, c)
        return (x, z * RING + turn(y, step), c)

    place = {"x": x, "y": y, "z": z}
    other_core = (x, row, 1 - c)

    quarter = hid_size // RING

    def quarter_of(i):
        return pl.ds(pl.multiple_of(i * quarter, quarter), quarter)

    w_out_copies = [
        pltpu.make_async_copy(
            w_out.at[:, pl.ds(start // RING, width // RING)],
            w_out_v.at[:, pl.ds(start // RING, width // RING)],
            local_sems.at[k],
        )
        for k, (start, width) in enumerate(zip(starts, WIDTHS))
    ]
    w_in_copy = pltpu.make_async_copy(w_in.at[:, quarter_of(x)], w_in_v, local_sems.at[len(WIDTHS)])
    cot_copy = pltpu.make_async_copy(cot, cot_v.at[c], local_sems.at[len(WIDTHS) + 1])
    acts_copy = pltpu.make_async_copy(acts, acts_in, local_sems.at[len(WIDTHS) + 2])
    pre_copy = pltpu.make_async_copy(pre, pre_v, local_sems.at[len(WIDTHS) + 3])
    for copy in (cot_copy, acts_copy, pre_copy):
        copy.start()

    partners = [at("x", 1), at("x", 2), at("x", 3), other_core]
    partners += [(turn(x, s), row, 1 - c) for s in (1, 2, 3)]
    partners += [at(axis, s) for axis in "zy" for s in (1, 2, 3)]
    barrier = pltpu.get_barrier_semaphore()
    for who in partners:
        pl.semaphore_signal(barrier, inc=1, device_id=who, device_id_type=MESH)

    for copy in w_out_copies:
        copy.start()

    acts_copy.wait()
    turned = acts_in[...].astype(F32).T.astype(BF16)
    lanes = pl.ds(pl.multiple_of(c * toks, toks), toks)
    for j in range(RING):
        acts_v[turn(j - x, RING), :, lanes] = turned[j * rows:(j + 1) * rows]
    cot_copy.wait()
    pl.semaphore_wait(barrier, len(partners))

    copies = Copies(send_sems, recv_sems)
    send = copies.send
    cot_core = send(cot_v.at[c], cot_v.at[c], other_core)
    w_in_copy.start()

    pre_copy.wait()

    @pl.loop(0, hid_size // TILE)
    def _(n):
        cols = pl.ds(pl.multiple_of(n * TILE, TILE), TILE)
        gelu, slope = gelu_and_slope(pre_v[:, cols].astype(F32))
        hid_v[:, cols] = gelu.astype(BF16)
        slope_v[:, cols] = slope * (1.0 / SHIFT)

    cot_core.wait_recv()
    cot_scaled[...] = cot_v[...] * jnp.array(SHIFT, BF16)
    early = {}

    def side():
        early["hid"] = [
            send(hid_v.at[:, quarter_of(turn(x, s))], hid_full.at[x, z, y], at("x", s))
            for s in (1, 3, 2)
        ]
        early["acts"] = send(acts_v.at[:, :, lanes], acts_v.at[:, :, lanes], other_core)
        hid_full[x, z, y] = hid_v[:, quarter_of(x)]
        yield
        early["acts_x"] = []
        for s in (1, 3, 2):
            for where in (at("x", s), (turn(x, s), row, 1 - c)):
                mine = acts_v.at[:, :, lanes]
                early["acts_x"].append(send(mine, acts_x.at[s - 1, :, :, lanes], where))
        yield
        early["cot"] = []
        for s in (1, 3, 2):
            for where in (at("x", s), (turn(x, s), row, 1 - c)):
                early["cot"].append(send(cot_v.at[c], cot_full.at[x, c], where))
        cot_full[x] = cot_v[...]

    def settle(keep):
        while len(copies.all) - copies.settled > keep:
            copies.all[copies.settled].wait_send()
            copies.settled += 1

    def gather(axis, source):
        i = place[axis]
        up, down = at(axis, 1), at(axis, 3)
        low, high = pl.ds(0, RING // 2), pl.ds(RING // 2, RING // 2)

        def push(i, depths, where):
            what = source(i).at[depths]
            return send(what, what, where)

        ups, downs = push(i, low, up), push(i, high, down)
        rest = [push(i, high, up), push(i, low, down)]
        yield
        ups.wait_recv()
        downs.wait_recv()
        rest.append(push(turn(i, 3), low, up))
        rest.append(push(turn(i, 1), high, down))
        yield
        for copy in rest:
            copy.wait_recv()

    def once(name, wait):
        if name not in early:
            early[name] = True
            wait()

    done = []

    def all_acts():
        early["acts"].wait_recv()
        for copy in early["acts_x"]:
            copy.wait_recv()
        acts_all[:, :, :2 * toks] = acts_v[...]
        for s in range(1, RING):
            there = slice(s * 2 * toks, (s + 1) * 2 * toks)
            acts_all[:RING - s, :, there] = acts_x[s - 1, s:]
            acts_all[RING - s:, :, there] = acts_x[s - 1, :s]

    def add_grad_in(start, width):
        once("w_in", w_in_copy.wait)
        cols = pl.ds(start, width)
        total = nt(gq[:, :, :, :, cols].reshape(-1, width), w_in_v[:, cols])
        total = total.reshape(gi.shape)
        early["summed"] = early.get("summed", 0) + width
        gi[...] = total if early["summed"] == width else gi[...] + total
        if early["summed"] == quarter:
            early["gi"] = send(gi.at[:, 1 - c], gi_recv, other_core)

    def grad_in_sum():
        early["gi"].wait_recv()
        gi_out[...] = gi[0, c] + gi_recv[0]
        gi_sum[...] = (gi[1:, c] + gi_recv[1:]).astype(BF16)
        finals = [send(gi_sum.at[s - 1], gi_depth.at[s - 1], at("x", -s)) for s in (2, 1, 3)]
        yield
        for copy in finals:
            copy.wait_recv()
        for s in range(RING - 1):
            gi_out[...] += gi_depth[s].astype(F32)

    def chunk(k):
        first, second = ("z", "y") if k % 2 == 0 else ("y", "z")
        a, b = place[first], place[second]
        start, width = starts[k], WIDTHS[k]
        half, size, q_start = width // 2, width // RING, start // RING
        cols, low, high = pl.ds(start, width), pl.ds(start, half), pl.ds(start + half, half)
        halves, q_cols = pl.ds(start // 2, half), pl.ds(q_start, size)

        def block(ref, i):
            return ref.at[i] if first == "z" else ref.at[:, i]

        def part_of(i):
            return pl.ds(pl.multiple_of(i * quarter + q_start, 128), size)

        w_out_copies[k].wait()
        weights = w_out_v[:, q_cols, :].reshape(width, feats)
        total = nt(cot_scaled[...].reshape(2 * toks, feats), weights)
        total = total.reshape(RING, RING, -1, width)
        part[:, :, :, cols] = total
        part16[:, :, :, cols] = coded(total)
        yield

        up, down = at(first, 1), at(first, 3)
        across, ahead, behind = turn(a, 2), turn(a, 1), turn(a, 3)
        relays = [
            send(block(part16, across).at[..., low], relay1.at[0, :, :, halves], up),
            send(block(part16, across).at[..., high], relay1.at[1, :, :, halves], down),
        ]
        finals = [
            send(block(part16, ahead).at[..., high], final1.at[0, :, :, high], up),
            send(block(part16, behind).at[..., low], final1.at[1, :, :, low], down),
        ]
        yield
        for n, (part_cols, i, where) in enumerate(((low, ahead, up), (high, behind, down))):
            relays[n].wait_recv()
            mine = block(part16, i).at[..., part_cols]
            mine[...] = coded(
                block(part, i)[..., part_cols] + decoded(relay1[n, :, :, halves])
            )
            finals.append(send(mine, final1.at[n, :, :, part_cols], where))
        yield
        for copy in finals:
            copy.wait_recv()
        total = block(part, a)[..., cols]
        total += decoded(final1[0, :, :, cols]) + decoded(final1[1, :, :, cols])
        mid[:, :, cols] = total
        mid16[:, :, cols] = coded(total)

        finals = [
            send(mid16.at[turn(b, s), :, cols], final2.at[s - 1, :, cols], at(second, s))
            for s in (2, 1, 3)
        ]
        yield
        for copy in finals:
            copy.wait_recv()
        grad_act = mid[b, :, cols]
        for n in range(RING - 1):
            grad_act += decoded(final2[n, :, cols])
        slope = jnp.concatenate(
            [slope_v[:, pl.ds(i * quarter + q_start, size)] for i in range(RING)], axis=1
        )
        gp[:, cols] = (grad_act * slope).astype(BF16)

        def mine_of(i):
            return pl.ds(pl.multiple_of(start + i * size, 128), size)

        swap = [
            send(gp.at[:, mine_of(turn(x, s))], gq.at[s, z, y, :, q_cols], at("x", s))
            for s in (2, 1, 3)
        ]
        gq[0, z, y, :, q_cols] = gp[:, mine_of(x)]
        yield
        for copy in swap:
            copy.wait_recv()

        mine = gq.at[:, z, y, :, q_cols]
        finals = [send(mine, mine, at(second, s)) for s in (2, 1, 3)]
        yield
        for copy in finals:
            copy.wait_recv()

        def rows_of(i):
            return (gq.at[:, i] if first == "z" else gq.at[:, :, i]).at[..., q_cols]

        yield from gather(first, rows_of)

        once("acts_all", all_acts)
        total = nn(
            acts_all[...].reshape(feats, -1), gq[:, :, :, :, q_cols].reshape(-1, size)
        )
        gwi_out[:, part_of(x)] = total[:rows] * norm_factor
        finals = []
        for j in (2, 1, 3):
            xpart[j - 1, :, q_cols] = total[j * rows:(j + 1) * rows].astype(BF16)
            finals.append(
                send(xpart.at[j - 1, :, q_cols], gwi_recv.at[:, part_of(x)], at("x", j))
            )
        yield
        if (k ^ 1) in done:
            add_grad_in(starts[k & ~1] // RING, (WIDTHS[k ^ 1] + width) // RING)
        done.append(k)
        yield
        settle(30)
        for copy in finals:
            copy.wait_recv()
        for j in range(1, RING):
            there = part_of(turn(x, j))
            gwi_out[:, there] = gwi_recv[:, there].astype(F32) * norm_factor

    def hidden(n):
        first, second = ("y", "z") if n == 0 else ("z", "y")
        size = quarter // 2
        mine = pl.ds(n * size, size)

        def line(i):
            return (hid_full.at[:, i, y] if first == "z" else hid_full.at[:, z, i]).at[..., mine]

        def plane(i):
            return (hid_full.at[:, i] if second == "z" else hid_full.at[:, :, i]).at[..., mine]

        def arrived(name):
            for copy in early[name]:
                copy.wait_recv()

        once("hid_there", functools.partial(arrived, "hid"))
        yield from gather(first, line)
        yield from gather(second, plane)
        yield
        once("cot_there", functools.partial(arrived, "cot"))
        total = tn(
            hid_full[:, :, :, :, mine].reshape(-1, size), cot_full[...].reshape(-1, feats)
        )
        gwo_out[mine, :] = total * norm_factor

    work = [chunk(k) for k in range(len(WIDTHS))] + [hidden(n) for n in range(2)] + [side(), grad_in_sum()]
    for i in ORDER:
        next(work[i], None)
    assert all(next(left, "done") == "done" for left in work)

    settle(0)
    assert len(copies.all) == n_copies, len(copies.all)


def store(*refs):
    sems = refs[-1]
    copies = [pltpu.make_async_copy(refs[i], refs[3 + i], sems.at[i]) for i in range(3)]
    for copy in copies:
        copy.start()
    for copy in copies:
        copy.wait()


def on_device(acts, cotangent, pre_act, w_in, w_out):
    hid, feats = w_out.shape
    toks, few = acts.shape[0], pre_act.shape[0]
    rows = feats // RING
    quarter = hid // RING
    quarters = (RING, RING, RING, few, quarter)
    n_copies = 24 * len(WIDTHS) + 45
    any_, vmem = pl.BlockSpec(memory_space=pl.ANY), pl.BlockSpec(memory_space=pltpu.VMEM)
    plane = (RING, few, hid)
    whole = (RING, RING, few, hid)
    norm_factor = 1.0 / math.sqrt(2 * toks * lax.axis_size("depth"))
    grad_in, grad_w_in, grad_w_out = pl.pallas_call(
        functools.partial(kernel, n_copies, norm_factor),
        out_shape=[
            pltpu.VMEM((toks, feats), F32),
            pltpu.VMEM((rows, hid), F32),
            pltpu.VMEM((hid // RING, feats), F32),
        ],
        in_specs=[any_] * 5,
        out_specs=[vmem] * 3,
        scratch_shapes=[
            pltpu.VMEM(quarters, BF16),
            pltpu.VMEM((toks, feats), BF16),
            pltpu.VMEM((few, hid), BF16),
            pltpu.VMEM((feats, quarter), BF16),
            pltpu.VMEM((RING, quarter, feats), BF16),
            pltpu.VMEM((2, toks, feats), BF16),
            pltpu.VMEM((2, toks, feats), BF16),
            pltpu.VMEM((RING, 2, toks, feats), BF16),
            pltpu.VMEM((rows, hid), BF16),
            pltpu.VMEM((RING, 2, toks, feats), F32),
            pltpu.VMEM((RING, toks, feats), F32),
            pltpu.VMEM((RING - 1, toks, feats), BF16),
            pltpu.VMEM((RING - 1, toks, feats), BF16),
            pltpu.VMEM((RING, rows, 2 * toks), BF16),
            pltpu.VMEM((RING - 1, RING, rows, 2 * toks), BF16),
            pltpu.VMEM((RING, rows, RING * 2 * toks), BF16),
            pltpu.VMEM((few, hid), F32),
            pltpu.VMEM((few, hid), BF16),
            pltpu.VMEM(whole, F32),
            pltpu.VMEM(whole, BF16),
            pltpu.VMEM((2, RING, few, hid // 2), BF16),
            pltpu.VMEM((2,) + plane, BF16),
            pltpu.VMEM(plane, F32),
            pltpu.VMEM(plane, BF16),
            pltpu.VMEM((RING - 1, few, hid), BF16),
            pltpu.VMEM((few, hid), BF16),
            pltpu.VMEM(quarters, BF16),
            pltpu.VMEM((RING - 1, rows, quarter), BF16),
            pltpu.SemaphoreType.DMA((n_copies,)),
            pltpu.SemaphoreType.DMA((n_copies,)),
            pltpu.SemaphoreType.DMA((len(WIDTHS) + 4,)),
        ],
        compiler_params=pltpu.CompilerParams(
            collective_id=0, has_side_effects=True, vmem_limit_bytes=52 * 2**20
        ),
        cost_estimate=pl.CostEstimate(
            flops=6 * 2 * toks * feats * hid, bytes_accessed=20 * 2**20, transcendentals=few * hid
        ),
        name="backward",
    )(acts, cotangent, pre_act, w_in, w_out.reshape(RING, quarter, feats))
    outs = (grad_in, grad_w_in, grad_w_out)
    grad_in, grad_w_in, grad_w_out = pl.pallas_call(
        store,
        out_shape=[jax.ShapeDtypeStruct(out.shape, F32) for out in outs],
        in_specs=[vmem] * 3,
        out_specs=[any_] * 3,
        scratch_shapes=[pltpu.SemaphoreType.DMA((3,))],
        compiler_params=pltpu.CompilerParams(vmem_limit_bytes=4 * 2**20),
        name="store",
    )(*[pltpu.with_memory_space_constraint(out, pltpu.VMEM) for out in outs])
    return grad_in, grad_w_in[None, None], grad_w_out[None, None]


def solution(mesh):
    in_specs = (
        P(("depth", "col"), "row"),
        P(("depth", "col"), "row"),
        P(("depth", "row"), "col"),
        P("row", "col"),
        P("col", "row"),
    )
    out_specs = (
        P(("depth", "col"), "row"),
        P("row", "depth", None, "col"),
        P("col", "depth", None, "row"),
    )
    return jax.shard_map(
        on_device, mesh=mesh, in_specs=in_specs, out_specs=out_specs, check_vma=False
    )
```

```python
import functools
import math

import jax
import jax.numpy as jnp
from jax import lax
from jax.experimental import pallas as pl
from jax.experimental.pallas import tpu as pltpu
from jax.sharding import PartitionSpec as P

MESH = pl.DeviceIdType.MESH
F32, BF16 = jnp.float32, jnp.bfloat16
RING = 4
WIDTHS = (1024, 1024, 1024, 1024, 1024, 1024)
PIECES = (768, 768)
ORDER = (
    1, 1, 0, 0, 5, 2, 8, 5, 2, 4, 3, 0, 3, 4, 8, 2, 1, 3, 5, 0, 4, 1, 3, 2, 5, 4, 6, 7, 0, 1, 2, 3,
    4, 7, 5, 0, 1, 6, 2, 3, 5, 4, 0, 1, 2, 8, 5, 4, 1, 2, 3, 5, 4, 0, 1, 3, 7, 6, 2, 4, 5, 0, 4, 3,
    0, 1, 5, 3, 2, 6, 2, 7, 9, 5, 1, 7, 0, 4, 7, 6, 3, 6, 9,
)
TILE = 768

gelu_coef = 0.044715
root = math.sqrt(2.0 / math.pi)


def gelu_and_slope(v):
    tanh_u = jnp.tanh(root * (v + gelu_coef * v * v * v))
    gelu = 0.5 * v * (1.0 + tanh_u)
    slope = 0.5 * (1.0 + tanh_u) + 0.5 * v * (1.0 - tanh_u * tanh_u) * root * (
        1.0 + 3.0 * gelu_coef * v * v
    )
    return gelu, slope


def nt(left, right):
    return lax.dot_general(
        left, right, (((1,), (1,)), ((), ())), preferred_element_type=F32
    )


def nn(left, right):
    return lax.dot_general(
        left, right, (((1,), (0,)), ((), ())), preferred_element_type=F32
    )


SHIFT = 2.0**20


def coded(v):
    v = v * jnp.abs(v)
    return (v * jnp.abs(v)).astype(BF16)


def decoded(t):
    t = t.astype(F32)
    r = lax.rsqrt(jnp.maximum(jnp.abs(t), 1e-37))
    return (t * r) * (r * lax.rsqrt(r))


def tn(left, right):
    return lax.dot_general(
        left, right, (((0,), (0,)), ((), ())), preferred_element_type=F32
    )


class Copies:
    def __init__(self, send_sems, recv_sems):
        self.send_sems, self.recv_sems = send_sems, recv_sems
        self.all, self.settled = [], 0

    def send(self, src, dst, to):
        n = len(self.all)
        copy = pltpu.make_async_remote_copy(
            src_ref=src,
            dst_ref=dst,
            send_sem=self.send_sems.at[n],
            recv_sem=self.recv_sems.at[n],
            device_id=to,
            device_id_type=MESH,
        )
        copy.start()
        self.all.append(copy)
        return copy


def kernel(
    n_copies, norm_factor, acts, cot, pre, w_in, w_out,
    gi_out, gwi_out, gwo_out,
    hid_full, acts_in, pre_v, w_in_v, w_out_v, cot_v, cot_scaled, cot_full, gwi_recv, gi, gi_recv, gi_sum, gi_depth,
    acts_v, acts_x, acts_all, slope_v, hid_v,
    part, part16, relay1, final1, mid, mid16, final2, gp, gq, xpart,
    send_sems, recv_sems, local_sems,
):
    x, row, c = lax.axis_index("depth"), lax.axis_index("row"), lax.axis_index("col")
    z, y = row // RING, row % RING
    feats, hid_size = w_in.shape
    toks, rows = acts.shape[0], feats // RING
    starts = [sum(WIDTHS[:k]) for k in range(len(WIDTHS))]

    def turn(i, step):
        return lax.rem(i + (step + RING), RING)

    def at(axis, step):
        if axis == "x":
            return (turn(x, step), row, c)
        if axis == "z":
            return (x, turn(z, step) * RING + y, c)
        return (x, z * RING + turn(y, step), c)

    place = {"x": x, "y": y, "z": z}
    other_core = (x, row, 1 - c)

    quarter = hid_size // RING

    def quarter_of(i):
        return pl.ds(pl.multiple_of(i * quarter, quarter), quarter)

    w_out_copies = [
        pltpu.make_async_copy(
            w_out.at[:, pl.ds(start // RING, width // RING)],
            w_out_v.at[:, pl.ds(start // RING, width // RING)],
            local_sems.at[k],
        )
        for k, (start, width) in enumerate(zip(starts, WIDTHS))
    ]
    w_in_copy = pltpu.make_async_copy(w_in.at[:, quarter_of(x)], w_in_v, local_sems.at[len(WIDTHS)])
    cot_copy = pltpu.make_async_copy(cot, cot_v.at[c], local_sems.at[len(WIDTHS) + 1])
    acts_copy = pltpu.make_async_copy(acts, acts_in, local_sems.at[len(WIDTHS) + 2])
    pre_copy = pltpu.make_async_copy(pre, pre_v, local_sems.at[len(WIDTHS) + 3])
    for copy in (cot_copy, acts_copy, pre_copy):
        copy.start()

    partners = [at("x", 1), at("x", 2), at("x", 3), other_core]
    partners += [(turn(x, s), row, 1 - c) for s in (1, 2, 3)]
    partners += [at(axis, s) for axis in "zy" for s in (1, 2, 3)]
    barrier = pltpu.get_barrier_semaphore()
    for who in partners:
        pl.semaphore_signal(barrier, inc=1, device_id=who, device_id_type=MESH)

    for copy in w_out_copies:
        copy.start()

    acts_copy.wait()
    turned = acts_in[...].astype(F32).T.astype(BF16)
    lanes = pl.ds(pl.multiple_of(c * toks, toks), toks)
    for j in range(RING):
        acts_v[turn(j - x, RING), :, lanes] = turned[j * rows:(j + 1) * rows]
    cot_copy.wait()
    pl.semaphore_wait(barrier, len(partners))

    copies = Copies(send_sems, recv_sems)
    send = copies.send
    cot_core = send(cot_v.at[c], cot_v.at[c], other_core)
    w_in_copy.start()

    pre_copy.wait()

    @pl.loop(0, hid_size // TILE)
    def _(n):
        cols = pl.ds(pl.multiple_of(n * TILE, TILE), TILE)
        gelu, slope = gelu_and_slope(pre_v[:, cols].astype(F32))
        hid_v[:, cols] = gelu.astype(BF16)
        slope_v[:, cols] = slope * (1.0 / SHIFT)

    early = {}
    early["hid"] = [
        send(hid_v.at[:, quarter_of(turn(x, s))], hid_full.at[x, z, y], at("x", s))
        for s in (2, 1, 3)
    ]
    hid_full[x, z, y] = hid_v[:, quarter_of(x)]
    cot_core.wait_recv()
    cot_scaled[...] = cot_v[...] * jnp.array(SHIFT, BF16)

    def side():
        early["acts"] = send(acts_v.at[:, :, lanes], acts_v.at[:, :, lanes], other_core)
        yield
        early["acts_x"] = []
        for s in (1, 3, 2):
            for where in (at("x", s), (turn(x, s), row, 1 - c)):
                mine = acts_v.at[:, :, lanes]
                early["acts_x"].append(send(mine, acts_x.at[s - 1, :, :, lanes], where))
        yield
        early["cot"] = []
        for s in (1, 3, 2):
            for where in (at("x", s), (turn(x, s), row, 1 - c)):
                early["cot"].append(send(cot_v.at[c], cot_full.at[x, c], where))
        cot_full[x] = cot_v[...]

    def settle(keep):
        while len(copies.all) - copies.settled > keep:
            copies.all[copies.settled].wait_send()
            copies.settled += 1

    def gather(axis, source):
        i = place[axis]
        up, down = at(axis, 1), at(axis, 3)
        low, high = pl.ds(0, RING // 2), pl.ds(RING // 2, RING // 2)

        def push(i, depths, where):
            what = source(i).at[depths]
            return send(what, what, where)

        ups, downs = push(i, low, up), push(i, high, down)
        rest = [push(i, high, up), push(i, low, down)]
        yield
        ups.wait_recv()
        downs.wait_recv()
        rest.append(push(turn(i, 3), low, up))
        rest.append(push(turn(i, 1), high, down))
        yield
        for copy in rest:
            copy.wait_recv()

    def once(name, wait):
        if name not in early:
            early[name] = True
            wait()

    done = []

    def all_acts():
        early["acts"].wait_recv()
        for copy in early["acts_x"]:
            copy.wait_recv()
        acts_all[:, :, :2 * toks] = acts_v[...]
        for s in range(1, RING):
            there = slice(s * 2 * toks, (s + 1) * 2 * toks)
            acts_all[:RING - s, :, there] = acts_x[s - 1, s:]
            acts_all[RING - s:, :, there] = acts_x[s - 1, :s]

    def add_grad_in(start, width):
        once("w_in", w_in_copy.wait)
        cols = pl.ds(start, width)
        total = nt(gq[:, :, :, :, cols].reshape(-1, width), w_in_v[:, cols])
        total = total.reshape(gi.shape)
        early["summed"] = early.get("summed", 0) + width
        gi[...] = total if early["summed"] == width else gi[...] + total
        if early["summed"] == quarter:
            early["gi"] = send(gi.at[:, 1 - c], gi_recv, other_core)

    def grad_in_sum():
        early["gi"].wait_recv()
        gi_out[...] = gi[0, c] + gi_recv[0]
        gi_sum[...] = (gi[1:, c] + gi_recv[1:]).astype(BF16)
        finals = [send(gi_sum.at[s - 1], gi_depth.at[s - 1], at("x", -s)) for s in (2, 1, 3)]
        yield
        for copy in finals:
            copy.wait_recv()
        for s in range(RING - 1):
            gi_out[...] += gi_depth[s].astype(F32)

    def chunk(k):
        first, second = ("z", "y") if k % 2 == 0 else ("y", "z")
        a, b = place[first], place[second]
        start, width = starts[k], WIDTHS[k]
        half, size, q_start = width // 2, width // RING, start // RING
        cols, low, high = pl.ds(start, width), pl.ds(start, half), pl.ds(start + half, half)
        halves, q_cols = pl.ds(start // 2, half), pl.ds(q_start, size)

        def block(ref, i):
            return ref.at[i] if first == "z" else ref.at[:, i]

        def part_of(i):
            return pl.ds(pl.multiple_of(i * quarter + q_start, 128), size)

        w_out_copies[k].wait()
        weights = w_out_v[:, q_cols, :].reshape(width, feats)
        total = nt(cot_scaled[...].reshape(2 * toks, feats), weights)
        total = total.reshape(RING, RING, -1, width)
        part[:, :, :, cols] = total
        part16[:, :, :, cols] = coded(total)
        yield

        up, down = at(first, 1), at(first, 3)
        across, ahead, behind = turn(a, 2), turn(a, 1), turn(a, 3)
        relays = [
            send(block(part16, across).at[..., low], relay1.at[0, :, :, halves], up),
            send(block(part16, across).at[..., high], relay1.at[1, :, :, halves], down),
        ]
        finals = [
            send(block(part16, ahead).at[..., high], final1.at[0, :, :, high], up),
            send(block(part16, behind).at[..., low], final1.at[1, :, :, low], down),
        ]
        yield
        for n, (part_cols, i, where) in enumerate(((low, ahead, up), (high, behind, down))):
            relays[n].wait_recv()
            mine = block(part16, i).at[..., part_cols]
            mine[...] = coded(
                block(part, i)[..., part_cols] + decoded(relay1[n, :, :, halves])
            )
            finals.append(send(mine, final1.at[n, :, :, part_cols], where))
        yield
        for copy in finals:
            copy.wait_recv()
        total = block(part, a)[..., cols]
        total += decoded(final1[0, :, :, cols]) + decoded(final1[1, :, :, cols])
        mid[:, :, cols] = total
        mid16[:, :, cols] = coded(total)

        finals = [
            send(mid16.at[turn(b, s), :, cols], final2.at[s - 1, :, cols], at(second, s))
            for s in (2, 1, 3)
        ]
        yield
        for copy in finals:
            copy.wait_recv()
        grad_act = mid[b, :, cols]
        for n in range(RING - 1):
            grad_act += decoded(final2[n, :, cols])
        slope = jnp.concatenate(
            [slope_v[:, pl.ds(i * quarter + q_start, size)] for i in range(RING)], axis=1
        )
        gp[:, cols] = (grad_act * slope).astype(BF16)

        def mine_of(i):
            return pl.ds(pl.multiple_of(start + i * size, 128), size)

        swap = [
            send(gp.at[:, mine_of(turn(x, s))], gq.at[s, z, y, :, q_cols], at("x", s))
            for s in (2, 1, 3)
        ]
        gq[0, z, y, :, q_cols] = gp[:, mine_of(x)]
        yield
        for copy in swap:
            copy.wait_recv()

        mine = gq.at[:, z, y, :, q_cols]
        finals = [send(mine, mine, at(second, s)) for s in (2, 1, 3)]
        yield
        for copy in finals:
            copy.wait_recv()

        def rows_of(i):
            return (gq.at[:, i] if first == "z" else gq.at[:, :, i]).at[..., q_cols]

        yield from gather(first, rows_of)

        once("acts_all", all_acts)
        total = nn(
            acts_all[...].reshape(feats, -1), gq[:, :, :, :, q_cols].reshape(-1, size)
        )
        gwi_out[:, part_of(x)] = total[:rows] * norm_factor
        finals = []
        for j in (2, 1, 3):
            xpart[j - 1, :, q_cols] = total[j * rows:(j + 1) * rows].astype(BF16)
            finals.append(
                send(xpart.at[j - 1, :, q_cols], gwi_recv.at[:, part_of(x)], at("x", j))
            )
        yield
        if (k ^ 1) in done:
            add_grad_in(starts[k & ~1] // RING, (WIDTHS[k ^ 1] + width) // RING)
        done.append(k)
        yield
        settle(30)
        for copy in finals:
            copy.wait_recv()
        for j in range(1, RING):
            there = part_of(turn(x, j))
            gwi_out[:, there] = gwi_recv[:, there].astype(F32) * norm_factor

    def hidden(n):
        first, second = ("y", "z") if n % 2 == 0 else ("z", "y")
        size = PIECES[n]
        mine = pl.ds(sum(PIECES[:n]), size)

        def line(i):
            return (hid_full.at[:, i, y] if first == "z" else hid_full.at[:, z, i]).at[..., mine]

        def plane(i):
            return (hid_full.at[:, i] if second == "z" else hid_full.at[:, :, i]).at[..., mine]

        def arrived(name):
            for copy in early[name]:
                copy.wait_recv()

        once("hid_there", functools.partial(arrived, "hid"))
        yield from gather(first, line)
        yield from gather(second, plane)
        yield
        once("cot_there", functools.partial(arrived, "cot"))
        total = tn(
            hid_full[:, :, :, :, mine].reshape(-1, size), cot_full[...].reshape(-1, feats)
        )
        gwo_out[mine, :] = total * norm_factor

    work = [chunk(k) for k in range(len(WIDTHS))] + [hidden(n) for n in range(len(PIECES))] + [side(), grad_in_sum()]
    for i in ORDER:
        next(work[i], None)
    assert all(next(left, "done") == "done" for left in work)

    settle(0)
    assert len(copies.all) == n_copies, len(copies.all)


def store(*refs):
    sems = refs[-1]
    copies = []
    for src, dst in zip(refs[:3], refs[3:6]):
        rows = src.shape[0] // 4
        for n in range(4):
            piece = pl.ds(n * rows, rows)
            sem = sems.at[len(copies)]
            copies.append(pltpu.make_async_copy(src.at[piece], dst.at[piece], sem))
    for copy in copies:
        copy.start()
    for copy in copies:
        copy.wait()


def on_device(acts, cotangent, pre_act, w_in, w_out):
    hid, feats = w_out.shape
    toks, few = acts.shape[0], pre_act.shape[0]
    rows = feats // RING
    quarter = hid // RING
    quarters = (RING, RING, RING, few, quarter)
    n_copies = 24 * len(WIDTHS) + 12 * len(PIECES) + 21
    any_, vmem = pl.BlockSpec(memory_space=pl.ANY), pl.BlockSpec(memory_space=pltpu.VMEM)
    plane = (RING, few, hid)
    whole = (RING, RING, few, hid)
    norm_factor = 1.0 / math.sqrt(2 * toks * lax.axis_size("depth"))
    grad_in, grad_w_in, grad_w_out = pl.pallas_call(
        functools.partial(kernel, n_copies, norm_factor),
        out_shape=[
            pltpu.VMEM((toks, feats), F32),
            pltpu.VMEM((rows, hid), F32),
            pltpu.VMEM((hid // RING, feats), F32),
        ],
        in_specs=[any_] * 5,
        out_specs=[vmem] * 3,
        scratch_shapes=[
            pltpu.VMEM(quarters, BF16),
            pltpu.VMEM((toks, feats), BF16),
            pltpu.VMEM((few, hid), BF16),
            pltpu.VMEM((feats, quarter), BF16),
            pltpu.VMEM((RING, quarter, feats), BF16),
            pltpu.VMEM((2, toks, feats), BF16),
            pltpu.VMEM((2, toks, feats), BF16),
            pltpu.VMEM((RING, 2, toks, feats), BF16),
            pltpu.VMEM((rows, hid), BF16),
            pltpu.VMEM((RING, 2, toks, feats), F32),
            pltpu.VMEM((RING, toks, feats), F32),
            pltpu.VMEM((RING - 1, toks, feats), BF16),
            pltpu.VMEM((RING - 1, toks, feats), BF16),
            pltpu.VMEM((RING, rows, 2 * toks), BF16),
            pltpu.VMEM((RING - 1, RING, rows, 2 * toks), BF16),
            pltpu.VMEM((RING, rows, RING * 2 * toks), BF16),
            pltpu.VMEM((few, hid), F32),
            pltpu.VMEM((few, hid), BF16),
            pltpu.VMEM(whole, F32),
            pltpu.VMEM(whole, BF16),
            pltpu.VMEM((2, RING, few, hid // 2), BF16),
            pltpu.VMEM((2,) + plane, BF16),
            pltpu.VMEM(plane, F32),
            pltpu.VMEM(plane, BF16),
            pltpu.VMEM((RING - 1, few, hid), BF16),
            pltpu.VMEM((few, hid), BF16),
            pltpu.VMEM(quarters, BF16),
            pltpu.VMEM((RING - 1, rows, quarter), BF16),
            pltpu.SemaphoreType.DMA((n_copies,)),
            pltpu.SemaphoreType.DMA((n_copies,)),
            pltpu.SemaphoreType.DMA((len(WIDTHS) + 4,)),
        ],
        compiler_params=pltpu.CompilerParams(
            collective_id=0, has_side_effects=True, vmem_limit_bytes=52 * 2**20
        ),
        cost_estimate=pl.CostEstimate(
            flops=6 * 2 * toks * feats * hid, bytes_accessed=20 * 2**20, transcendentals=few * hid
        ),
        name="backward",
    )(acts, cotangent, pre_act, w_in, w_out.reshape(RING, quarter, feats))
    outs = (grad_in, grad_w_in, grad_w_out)
    grad_in, grad_w_in, grad_w_out = pl.pallas_call(
        store,
        out_shape=[jax.ShapeDtypeStruct(out.shape, F32) for out in outs],
        in_specs=[vmem] * 3,
        out_specs=[any_] * 3,
        scratch_shapes=[pltpu.SemaphoreType.DMA((12,))],
        compiler_params=pltpu.CompilerParams(vmem_limit_bytes=4 * 2**20),
        name="store",
    )(*[pltpu.with_memory_space_constraint(out, pltpu.VMEM) for out in outs])
    return grad_in, grad_w_in[None, None], grad_w_out[None, None]


def solution(mesh):
    in_specs = (
        P(("depth", "col"), "row"),
        P(("depth", "col"), "row"),
        P(("depth", "row"), "col"),
        P("row", "col"),
        P("col", "row"),
    )
    out_specs = (
        P(("depth", "col"), "row"),
        P("row", "depth", None, "col"),
        P("col", "depth", None, "row"),
    )
    return jax.shard_map(
        on_device, mesh=mesh, in_specs=in_specs, out_specs=out_specs, check_vma=False
    )
```

```python
import functools
import math

import jax
import jax.numpy as jnp
from jax import lax
from jax.experimental import pallas as pl
from jax.experimental.pallas import tpu as pltpu
from jax.sharding import PartitionSpec as P

MESH = pl.DeviceIdType.MESH
F32, BF16 = jnp.float32, jnp.bfloat16
RING = 4
WIDTHS = (1024, 1024, 1024, 1024, 1024, 1024)
PIECES = (768, 768)
ORDER = (
    2, 2, 5, 5, 3, 4, 4, 3, 2, 8, 8, 5, 4, 0, 3, 0, 1, 2, 5, 1, 3, 4, 0, 1, 7, 2, 5, 6, 0, 3, 1, 4,
    2, 6, 5, 7, 3, 1, 0, 4, 2, 5, 8, 1, 0, 4, 2, 5, 3, 4, 1, 5, 3, 0, 2, 4, 1, 7, 0, 2, 4, 5, 6, 3,
    3, 1, 1, 0, 0, 5, 2, 6, 3, 7, 9, 1, 0, 4, 7, 7, 6, 6, 9,
)
TILE = 768

gelu_coef = 0.044715
root = math.sqrt(2.0 / math.pi)


def gelu_and_slope(v):
    tanh_u = jnp.tanh(root * (v + gelu_coef * v * v * v))
    gelu = 0.5 * v * (1.0 + tanh_u)
    slope = 0.5 * (1.0 + tanh_u) + 0.5 * v * (1.0 - tanh_u * tanh_u) * root * (
        1.0 + 3.0 * gelu_coef * v * v
    )
    return gelu, slope


def nt(left, right):
    return lax.dot_general(
        left, right, (((1,), (1,)), ((), ())), preferred_element_type=F32
    )


def nn(left, right):
    return lax.dot_general(
        left, right, (((1,), (0,)), ((), ())), preferred_element_type=F32
    )


SHIFT = 2.0**20


def coded(v):
    v = v * jnp.abs(v)
    return (v * jnp.abs(v)).astype(BF16)


def decoded(t):
    t = t.astype(F32)
    r = lax.rsqrt(jnp.maximum(jnp.abs(t), 1e-37))
    return (t * r) * (r * lax.rsqrt(r))


def tn(left, right):
    return lax.dot_general(
        left, right, (((0,), (0,)), ((), ())), preferred_element_type=F32
    )


class Copies:
    def __init__(self, send_sems, recv_sems):
        self.send_sems, self.recv_sems = send_sems, recv_sems
        self.all, self.settled = [], 0

    def send(self, src, dst, to):
        n = len(self.all)
        copy = pltpu.make_async_remote_copy(
            src_ref=src,
            dst_ref=dst,
            send_sem=self.send_sems.at[n],
            recv_sem=self.recv_sems.at[n],
            device_id=to,
            device_id_type=MESH,
        )
        copy.start()
        self.all.append(copy)
        return copy


def kernel(
    n_copies, norm_factor, acts, cot, pre, w_in, w_out,
    gi_out, gwi_out, gwo_out,
    hid_full, acts_in, pre_v, w_in_v, w_out_v, cot_v, cot_scaled, cot_full, gwi_recv, gi, gi_recv, gi_sum, gi_depth,
    acts_v, acts_x, acts_all, slope_v, hid_v,
    part, part16, relay1, final1, mid, mid16, final2, gp, gq, xpart,
    send_sems, recv_sems, local_sems,
):
    x, row, c = lax.axis_index("depth"), lax.axis_index("row"), lax.axis_index("col")
    z, y = row // RING, row % RING
    feats, hid_size = w_in.shape
    toks, rows = acts.shape[0], feats // RING
    starts = [sum(WIDTHS[:k]) for k in range(len(WIDTHS))]

    def turn(i, step):
        return lax.rem(i + (step + RING), RING)

    def at(axis, step):
        if axis == "x":
            return (turn(x, step), row, c)
        if axis == "z":
            return (x, turn(z, step) * RING + y, c)
        return (x, z * RING + turn(y, step), c)

    place = {"x": x, "y": y, "z": z}
    other_core = (x, row, 1 - c)

    quarter = hid_size // RING

    def quarter_of(i):
        return pl.ds(pl.multiple_of(i * quarter, quarter), quarter)

    w_out_copies = [
        pltpu.make_async_copy(
            w_out.at[:, pl.ds(start // RING, width // RING)],
            w_out_v.at[:, pl.ds(start // RING, width // RING)],
            local_sems.at[k],
        )
        for k, (start, width) in enumerate(zip(starts, WIDTHS))
    ]
    w_in_copy = pltpu.make_async_copy(w_in.at[:, quarter_of(x)], w_in_v, local_sems.at[len(WIDTHS)])
    cot_copy = pltpu.make_async_copy(cot, cot_v.at[c], local_sems.at[len(WIDTHS) + 1])
    acts_copy = pltpu.make_async_copy(acts, acts_in, local_sems.at[len(WIDTHS) + 2])
    pre_copy = pltpu.make_async_copy(pre, pre_v, local_sems.at[len(WIDTHS) + 3])
    for copy in (cot_copy, acts_copy, pre_copy):
        copy.start()

    partners = [at("x", 1), at("x", 2), at("x", 3), other_core]
    partners += [(turn(x, s), row, 1 - c) for s in (1, 2, 3)]
    partners += [at(axis, s) for axis in "zy" for s in (1, 2, 3)]
    barrier = pltpu.get_barrier_semaphore()
    for who in partners:
        pl.semaphore_signal(barrier, inc=1, device_id=who, device_id_type=MESH)

    for copy in w_out_copies:
        copy.start()

    acts_copy.wait()
    turned = acts_in[...].astype(F32).T.astype(BF16)
    lanes = pl.ds(pl.multiple_of(c * toks, toks), toks)
    for j in range(RING):
        acts_v[turn(j - x, RING), :, lanes] = turned[j * rows:(j + 1) * rows]
    cot_copy.wait()
    pl.semaphore_wait(barrier, len(partners))

    copies = Copies(send_sems, recv_sems)
    send = copies.send
    cot_core = send(cot_v.at[c], cot_v.at[c], other_core)
    w_in_copy.start()

    pre_copy.wait()

    @pl.loop(0, hid_size // TILE)
    def _(n):
        cols = pl.ds(pl.multiple_of(n * TILE, TILE), TILE)
        gelu, slope = gelu_and_slope(pre_v[:, cols].astype(F32))
        hid_v[:, cols] = gelu.astype(BF16)
        slope_v[:, cols] = slope * (1.0 / SHIFT)

    early = {}
    early["hid"] = [
        send(hid_v.at[:, quarter_of(turn(x, s))], hid_full.at[x, z, y], at("x", s))
        for s in (2, 1, 3)
    ]
    hid_full[x, z, y] = hid_v[:, quarter_of(x)]
    cot_core.wait_recv()
    cot_scaled[...] = cot_v[...] * jnp.array(SHIFT, BF16)

    def side():
        early["acts"] = send(acts_v.at[:, :, lanes], acts_v.at[:, :, lanes], other_core)
        yield
        early["acts_x"] = []
        for s in (1, 3, 2):
            for where in (at("x", s), (turn(x, s), row, 1 - c)):
                mine = acts_v.at[:, :, lanes]
                early["acts_x"].append(send(mine, acts_x.at[s - 1, :, :, lanes], where))
        yield
        early["cot"] = []
        for s in (1, 3, 2):
            for where in (at("x", s), (turn(x, s), row, 1 - c)):
                early["cot"].append(send(cot_v.at[c], cot_full.at[x, c], where))
        cot_full[x] = cot_v[...]

    def settle(keep):
        while len(copies.all) - copies.settled > keep:
            copies.all[copies.settled].wait_send()
            copies.settled += 1

    def gather(axis, source):
        i = place[axis]
        up, down = at(axis, 1), at(axis, 3)
        low, high = pl.ds(0, RING // 2), pl.ds(RING // 2, RING // 2)

        def push(i, depths, where):
            what = source(i).at[depths]
            return send(what, what, where)

        ups, downs = push(i, low, up), push(i, high, down)
        rest = [push(i, high, up), push(i, low, down)]
        yield
        ups.wait_recv()
        downs.wait_recv()
        rest.append(push(turn(i, 3), low, up))
        rest.append(push(turn(i, 1), high, down))
        yield
        for copy in rest:
            copy.wait_recv()

    def once(name, wait):
        if name not in early:
            early[name] = True
            wait()

    done = []

    def all_acts():
        early["acts"].wait_recv()
        for copy in early["acts_x"]:
            copy.wait_recv()
        acts_all[:, :, :2 * toks] = acts_v[...]
        for s in range(1, RING):
            there = slice(s * 2 * toks, (s + 1) * 2 * toks)
            acts_all[:RING - s, :, there] = acts_x[s - 1, s:]
            acts_all[RING - s:, :, there] = acts_x[s - 1, :s]

    def add_grad_in(k):
        once("w_in", w_in_copy.wait)
        width = (WIDTHS[k] + WIDTHS[k + 1]) // RING
        pair = jnp.concatenate([gq[k], gq[k + 1]], axis=-1).reshape(-1, width)
        total = nt(pair, w_in_v[:, pl.ds(starts[k] // RING, width)])
        total = total.reshape(gi.shape)
        early["summed"] = early.get("summed", 0) + width
        gi[...] = total if early["summed"] == width else gi[...] + total
        if early["summed"] == quarter:
            early["gi"] = send(gi.at[:, 1 - c], gi_recv, other_core)

    def grad_in_sum():
        early["gi"].wait_recv()
        gi_out[...] = gi[0, c] + gi_recv[0]
        gi_sum[...] = (gi[1:, c] + gi_recv[1:]).astype(BF16)
        finals = [send(gi_sum.at[s - 1], gi_depth.at[s - 1], at("x", -s)) for s in (2, 1, 3)]
        yield
        for copy in finals:
            copy.wait_recv()
        for s in range(RING - 1):
            gi_out[...] += gi_depth[s].astype(F32)

    def chunk(k):
        first, second = ("z", "y") if k % 2 == 0 else ("y", "z")
        a, b = place[first], place[second]
        start, width = starts[k], WIDTHS[k]
        size, q_start = width // RING, start // RING
        cols, q_cols = pl.ds(start, width), pl.ds(q_start, size)
        low, high = pl.ds(0, RING // 2), pl.ds(RING // 2, RING // 2)

        def block(ref, i, half=slice(None)):
            return ref.at[k, i, half] if first == "z" else ref.at[k, half, i]

        def part_of(i):
            return pl.ds(pl.multiple_of(i * quarter + q_start, 128), size)

        w_out_copies[k].wait()
        weights = w_out_v[:, q_cols, :].reshape(width, feats)
        total = nt(cot_scaled[...].reshape(2 * toks, feats), weights)
        total = total.reshape(RING, RING, -1, width)
        part[k] = total
        part16[k] = coded(total)
        yield

        up, down = at(first, 1), at(first, 3)
        across, ahead, behind = turn(a, 2), turn(a, 1), turn(a, 3)
        relays = [
            send(block(part16, across, low), relay1.at[k, 0], up),
            send(block(part16, across, high), relay1.at[k, 1], down),
        ]
        finals = [
            send(block(part16, ahead, high), final1.at[k, 0, high], up),
            send(block(part16, behind, low), final1.at[k, 1, low], down),
        ]
        yield
        for n, (half, i, where) in enumerate(((low, ahead, up), (high, behind, down))):
            relays[n].wait_recv()
            mine = block(part16, i, half)
            mine[...] = coded(block(part, i, half)[...] + decoded(relay1[k, n]))
            finals.append(send(mine, final1.at[k, n, half], where))
        yield
        for copy in finals:
            copy.wait_recv()
        total = block(part, a)[...] + decoded(final1[k, 0]) + decoded(final1[k, 1])
        mid[k] = total
        mid16[k] = coded(total)

        finals = [
            send(mid16.at[k, turn(b, s)], final2.at[k, s - 1], at(second, s)) for s in (2, 1, 3)
        ]
        yield
        for copy in finals:
            copy.wait_recv()
        grad_act = mid[k, b]
        for n in range(RING - 1):
            grad_act += decoded(final2[k, n])
        for i in range(RING):
            slope = slope_v[:, pl.ds(i * quarter + q_start, size)]
            gp[k, i] = (grad_act[:, i * size:(i + 1) * size] * slope).astype(BF16)

        swap = [send(gp.at[k, turn(x, s)], gq.at[k, s, z, y], at("x", s)) for s in (2, 1, 3)]
        gq[k, 0, z, y] = gp[k, x]
        yield
        for copy in swap:
            copy.wait_recv()

        mine = gq.at[k, :, z, y]
        finals = [send(mine, mine, at(second, s)) for s in (2, 1, 3)]
        yield
        for copy in finals:
            copy.wait_recv()

        def rows_of(i):
            return gq.at[k, :, i] if first == "z" else gq.at[k, :, :, i]

        yield from gather(first, rows_of)

        once("acts_all", all_acts)
        total = nn(acts_all[...].reshape(feats, -1), gq[k].reshape(-1, size))
        gwi_out[:, part_of(x)] = total[:rows] * norm_factor
        finals = []
        for j in (2, 1, 3):
            xpart[k, j - 1] = total[j * rows:(j + 1) * rows].astype(BF16)
            finals.append(send(xpart.at[k, j - 1], gwi_recv.at[k, j - 1], at("x", j)))
        yield
        if (k ^ 1) in done:
            add_grad_in(k & ~1)
        done.append(k)
        yield
        settle(30)
        for copy in finals:
            copy.wait_recv()
        for j in range(1, RING):
            there = part_of(turn(x, -j))
            gwi_out[:, there] = gwi_recv[k, j - 1].astype(F32) * norm_factor

    def hidden(n):
        first, second = ("y", "z") if n % 2 == 0 else ("z", "y")
        size = PIECES[n]
        mine = pl.ds(sum(PIECES[:n]), size)

        def line(i):
            return (hid_full.at[:, i, y] if first == "z" else hid_full.at[:, z, i]).at[..., mine]

        def plane(i):
            return (hid_full.at[:, i] if second == "z" else hid_full.at[:, :, i]).at[..., mine]

        def arrived(name):
            for copy in early[name]:
                copy.wait_recv()

        once("hid_there", functools.partial(arrived, "hid"))
        yield from gather(first, line)
        yield from gather(second, plane)
        yield
        once("cot_there", functools.partial(arrived, "cot"))
        total = tn(
            hid_full[:, :, :, :, mine].reshape(-1, size), cot_full[...].reshape(-1, feats)
        )
        gwo_out[mine, :] = total * norm_factor

    work = [chunk(k) for k in range(len(WIDTHS))] + [hidden(n) for n in range(len(PIECES))] + [side(), grad_in_sum()]
    for i in ORDER:
        next(work[i], None)
    assert all(next(left, "done") == "done" for left in work)

    settle(0)
    assert len(copies.all) == n_copies, len(copies.all)


def store(*refs):
    sems = refs[-1]
    copies = []
    for src, dst in zip(refs[:3], refs[3:6]):
        rows = src.shape[0] // 4
        for n in range(4):
            piece = pl.ds(n * rows, rows)
            sem = sems.at[len(copies)]
            copies.append(pltpu.make_async_copy(src.at[piece], dst.at[piece], sem))
    for copy in copies:
        copy.start()
    for copy in copies:
        copy.wait()


def on_device(acts, cotangent, pre_act, w_in, w_out):
    hid, feats = w_out.shape
    toks, few = acts.shape[0], pre_act.shape[0]
    rows = feats // RING
    quarter = hid // RING
    quarters = (RING, RING, RING, few, quarter)
    n_copies = 24 * len(WIDTHS) + 12 * len(PIECES) + 21
    any_, vmem = pl.BlockSpec(memory_space=pl.ANY), pl.BlockSpec(memory_space=pltpu.VMEM)
    chunks, width = len(WIDTHS), WIDTHS[0]
    size, plane = width // RING, (RING, few, width)
    assert all(other == width for other in WIDTHS)
    norm_factor = 1.0 / math.sqrt(2 * toks * lax.axis_size("depth"))
    grad_in, grad_w_in, grad_w_out = pl.pallas_call(
        functools.partial(kernel, n_copies, norm_factor),
        out_shape=[
            pltpu.VMEM((toks, feats), F32),
            pltpu.VMEM((rows, hid), F32),
            pltpu.VMEM((hid // RING, feats), F32),
        ],
        in_specs=[any_] * 5,
        out_specs=[vmem] * 3,
        scratch_shapes=[
            pltpu.VMEM(quarters, BF16),
            pltpu.VMEM((toks, feats), BF16),
            pltpu.VMEM((few, hid), BF16),
            pltpu.VMEM((feats, quarter), BF16),
            pltpu.VMEM((RING, quarter, feats), BF16),
            pltpu.VMEM((2, toks, feats), BF16),
            pltpu.VMEM((2, toks, feats), BF16),
            pltpu.VMEM((RING, 2, toks, feats), BF16),
            pltpu.VMEM((chunks, RING - 1, rows, size), BF16),
            pltpu.VMEM((RING, 2, toks, feats), F32),
            pltpu.VMEM((RING, toks, feats), F32),
            pltpu.VMEM((RING - 1, toks, feats), BF16),
            pltpu.VMEM((RING - 1, toks, feats), BF16),
            pltpu.VMEM((RING, rows, 2 * toks), BF16),
            pltpu.VMEM((RING - 1, RING, rows, 2 * toks), BF16),
            pltpu.VMEM((RING, rows, RING * 2 * toks), BF16),
            pltpu.VMEM((few, hid), F32),
            pltpu.VMEM((few, hid), BF16),
            pltpu.VMEM((chunks, RING) + plane, F32),
            pltpu.VMEM((chunks, RING) + plane, BF16),
            pltpu.VMEM((chunks, 2, RING // 2) + plane[1:], BF16),
            pltpu.VMEM((chunks, 2) + plane, BF16),
            pltpu.VMEM((chunks,) + plane, F32),
            pltpu.VMEM((chunks,) + plane, BF16),
            pltpu.VMEM((chunks, RING - 1) + plane[1:], BF16),
            pltpu.VMEM((chunks, RING, few, size), BF16),
            pltpu.VMEM((chunks, RING, RING, RING, few, size), BF16),
            pltpu.VMEM((chunks, RING - 1, rows, size), BF16),
            pltpu.SemaphoreType.DMA((n_copies,)),
            pltpu.SemaphoreType.DMA((n_copies,)),
            pltpu.SemaphoreType.DMA((len(WIDTHS) + 4,)),
        ],
        compiler_params=pltpu.CompilerParams(
            collective_id=0, has_side_effects=True, vmem_limit_bytes=52 * 2**20
        ),
        cost_estimate=pl.CostEstimate(
            flops=6 * 2 * toks * feats * hid, bytes_accessed=20 * 2**20, transcendentals=few * hid
        ),
        name="backward",
    )(acts, cotangent, pre_act, w_in, w_out.reshape(RING, quarter, feats))
    outs = (grad_in, grad_w_in, grad_w_out)
    grad_in, grad_w_in, grad_w_out = pl.pallas_call(
        store,
        out_shape=[jax.ShapeDtypeStruct(out.shape, F32) for out in outs],
        in_specs=[vmem] * 3,
        out_specs=[any_] * 3,
        scratch_shapes=[pltpu.SemaphoreType.DMA((12,))],
        compiler_params=pltpu.CompilerParams(vmem_limit_bytes=4 * 2**20),
        name="store",
    )(*[pltpu.with_memory_space_constraint(out, pltpu.VMEM) for out in outs])
    return grad_in, grad_w_in[None, None], grad_w_out[None, None]


def solution(mesh):
    in_specs = (
        P(("depth", "col"), "row"),
        P(("depth", "col"), "row"),
        P(("depth", "row"), "col"),
        P("row", "col"),
        P("col", "row"),
    )
    out_specs = (
        P(("depth", "col"), "row"),
        P("row", "depth", None, "col"),
        P("col", "depth", None, "row"),
    )
    return jax.shard_map(
        on_device, mesh=mesh, in_specs=in_specs, out_specs=out_specs, check_vma=False
    )
```

```python
import functools
import math

import jax
import jax.numpy as jnp
from jax import lax
from jax.experimental import pallas as pl
from jax.experimental.pallas import tpu as pltpu
from jax.sharding import PartitionSpec as P

MESH = pl.DeviceIdType.MESH
F32, BF16 = jnp.float32, jnp.bfloat16
RING = 4
WIDTHS = (1024, 1024, 1024, 1024, 1024, 1024)
PIECES = (768, 768)
ORDER = (
    1, 1, 4, 4, 5, 0, 5, 3, 2, 2, 3, 0, 8, 8, 1, 4, 3, 0, 4, 1, 5, 3, 0, 2, 6, 4, 1, 5, 3, 7, 2, 0,
    4, 1, 3, 5, 7, 6, 2, 0, 4, 1, 5, 8, 2, 0, 1, 4, 3, 0, 5, 2, 1, 3, 4, 5, 7, 2, 0, 0, 6, 3, 1, 5,
    3, 4, 2, 2, 5, 7, 6, 4, 9, 7, 0, 3, 7, 6, 6, 9, 2, 5, 1,
)
TILE = 768

gelu_coef = 0.044715
root = math.sqrt(2.0 / math.pi)


def gelu_and_slope(v):
    tanh_u = jnp.tanh(root * (v + gelu_coef * v * v * v))
    gelu = 0.5 * v * (1.0 + tanh_u)
    slope = 0.5 * (1.0 + tanh_u) + 0.5 * v * (1.0 - tanh_u * tanh_u) * root * (
        1.0 + 3.0 * gelu_coef * v * v
    )
    return gelu, slope


def nt(left, right):
    return lax.dot_general(
        left, right, (((1,), (1,)), ((), ())), preferred_element_type=F32
    )


def nn(left, right):
    return lax.dot_general(
        left, right, (((1,), (0,)), ((), ())), preferred_element_type=F32
    )


SHIFT = 2.0**20


def coded(v):
    v = v * jnp.abs(v)
    return (v * jnp.abs(v)).astype(BF16)


def decoded(t):
    t = t.astype(F32)
    r = lax.rsqrt(jnp.maximum(jnp.abs(t), 1e-37))
    return (t * r) * (r * lax.rsqrt(r))


def tn(left, right):
    return lax.dot_general(
        left, right, (((0,), (0,)), ((), ())), preferred_element_type=F32
    )


class Copies:
    def __init__(self, send_sems, recv_sems):
        self.send_sems, self.recv_sems = send_sems, recv_sems
        self.all, self.settled = [], 0

    def send(self, src, dst, to):
        n = len(self.all)
        copy = pltpu.make_async_remote_copy(
            src_ref=src,
            dst_ref=dst,
            send_sem=self.send_sems.at[n],
            recv_sem=self.recv_sems.at[n],
            device_id=to,
            device_id_type=MESH,
        )
        copy.start()
        self.all.append(copy)
        return copy


def kernel(
    n_copies, norm_factor, acts, cot, pre, w_in, w_out,
    gi_out, gwi_out, gwo_out,
    hid_full, acts_in, pre_v, w_in_v, w_out_v, cot_v, cot_scaled, cot_full, gwi_recv, gi, gi_recv, gi_sum, gi_depth,
    acts_v, acts_x, acts_all, slope_v, hid_v,
    part, part16, relay1, final1, mid, mid16, final2, gp, gq, xpart,
    send_sems, recv_sems, local_sems,
):
    x, row, c = lax.axis_index("depth"), lax.axis_index("row"), lax.axis_index("col")
    z, y = row // RING, row % RING
    feats, hid_size = w_in.shape
    toks, rows = acts.shape[0], feats // RING
    starts = [sum(WIDTHS[:k]) for k in range(len(WIDTHS))]

    def turn(i, step):
        return lax.rem(i + (step + RING), RING)

    def at(axis, step):
        if axis == "x":
            return (turn(x, step), row, c)
        if axis == "z":
            return (x, turn(z, step) * RING + y, c)
        return (x, z * RING + turn(y, step), c)

    place = {"x": x, "y": y, "z": z}
    other_core = (x, row, 1 - c)

    quarter = hid_size // RING

    def quarter_of(i):
        return pl.ds(pl.multiple_of(i * quarter, quarter), quarter)

    w_out_copies = [
        pltpu.make_async_copy(
            w_out.at[:, pl.ds(start // RING, width // RING)],
            w_out_v.at[:, pl.ds(start // RING, width // RING)],
            local_sems.at[k],
        )
        for k, (start, width) in enumerate(zip(starts, WIDTHS))
    ]
    w_in_copy = pltpu.make_async_copy(w_in.at[:, quarter_of(x)], w_in_v, local_sems.at[len(WIDTHS)])
    cot_copy = pltpu.make_async_copy(cot, cot_v.at[c], local_sems.at[len(WIDTHS) + 1])
    acts_copy = pltpu.make_async_copy(acts, acts_in, local_sems.at[len(WIDTHS) + 2])
    pre_copy = pltpu.make_async_copy(pre, pre_v, local_sems.at[len(WIDTHS) + 3])

    partners = [other_core] + [at(axis, s) for axis in "zy" for s in (1, 2, 3)]
    partners += [(turn(x, s), row, core) for core in (c, 1 - c) for s in (1, 2, 3)]
    barrier = pltpu.get_barrier_semaphore()
    for who in partners:
        pl.semaphore_signal(barrier, inc=1, device_id=who, device_id_type=MESH)

    for copy in [cot_copy, pre_copy, *w_out_copies, acts_copy]:
        copy.start()
    lanes = pl.ds(pl.multiple_of(c * toks, toks), toks)
    cot_copy.wait()
    pl.semaphore_wait(barrier, len(partners))

    copies = Copies(send_sems, recv_sems)
    send = copies.send
    cot_core = send(cot_v.at[c], cot_v.at[c], other_core)
    w_in_copy.start()

    pre_copy.wait()

    @pl.loop(0, hid_size // TILE)
    def _(n):
        cols = pl.ds(pl.multiple_of(n * TILE, TILE), TILE)
        gelu, slope = gelu_and_slope(pre_v[:, cols].astype(F32))
        hid_v[:, cols] = gelu.astype(BF16)
        slope_v[:, cols] = slope * (1.0 / SHIFT)

    early = {}
    early["hid"] = [
        send(hid_v.at[:, quarter_of(turn(x, s))], hid_full.at[x, z, y], at("x", s))
        for s in (2, 1, 3)
    ]
    hid_full[x, z, y] = hid_v[:, quarter_of(x)]
    cot_core.wait_recv()
    cot_scaled[...] = cot_v[...] * jnp.array(SHIFT, BF16)

    def side():
        acts_copy.wait()
        turned = acts_in[...].astype(F32).T.astype(BF16)
        for j in range(RING):
            acts_v[turn(j - x, RING), :, lanes] = turned[j * rows:(j + 1) * rows]
        early["acts"] = send(acts_v.at[:, :, lanes], acts_v.at[:, :, lanes], other_core)
        yield
        early["acts_x"] = []
        for s in (1, 3, 2):
            for where in (at("x", s), (turn(x, s), row, 1 - c)):
                mine = acts_v.at[:, :, lanes]
                early["acts_x"].append(send(mine, acts_x.at[s - 1, :, :, lanes], where))
        yield
        early["cot"] = []
        for s in (1, 3, 2):
            for where in (at("x", s), (turn(x, s), row, 1 - c)):
                early["cot"].append(send(cot_v.at[c], cot_full.at[x, c], where))
        cot_full[x] = cot_v[...]

    def settle(keep):
        while len(copies.all) - copies.settled > keep:
            copies.all[copies.settled].wait_send()
            copies.settled += 1

    def gather(axis, source):
        i = place[axis]
        up, down = at(axis, 1), at(axis, 3)
        low, high = pl.ds(0, RING // 2), pl.ds(RING // 2, RING // 2)

        def push(i, depths, where):
            what = source(i).at[depths]
            return send(what, what, where)

        ups, downs = push(i, low, up), push(i, high, down)
        rest = [push(i, high, up), push(i, low, down)]
        yield
        ups.wait_recv()
        downs.wait_recv()
        rest.append(push(turn(i, 3), low, up))
        rest.append(push(turn(i, 1), high, down))
        yield
        for copy in rest:
            copy.wait_recv()

    def once(name, wait):
        if name not in early:
            early[name] = True
            wait()

    done = []

    def all_acts():
        early["acts"].wait_recv()
        for copy in early["acts_x"]:
            copy.wait_recv()
        acts_all[:, :, :2 * toks] = acts_v[...]
        for s in range(1, RING):
            there = slice(s * 2 * toks, (s + 1) * 2 * toks)
            acts_all[:RING - s, :, there] = acts_x[s - 1, s:]
            acts_all[RING - s:, :, there] = acts_x[s - 1, :s]

    def add_grad_in(k):
        once("w_in", w_in_copy.wait)
        width = (WIDTHS[k] + WIDTHS[k + 1]) // RING
        pair = jnp.concatenate([gq[k], gq[k + 1]], axis=-1).reshape(-1, width)
        total = nt(pair, w_in_v[:, pl.ds(starts[k] // RING, width)])
        total = total.reshape(gi.shape)
        early["summed"] = early.get("summed", 0) + width
        gi[...] = total if early["summed"] == width else gi[...] + total
        if early["summed"] == quarter:
            early["gi"] = send(gi.at[:, 1 - c], gi_recv, other_core)

    def grad_in_sum():
        early["gi"].wait_recv()
        gi_out[...] = gi[0, c] + gi_recv[0]
        gi_sum[...] = (gi[1:, c] + gi_recv[1:]).astype(BF16)
        finals = [send(gi_sum.at[s - 1], gi_depth.at[s - 1], at("x", -s)) for s in (2, 1, 3)]
        yield
        for copy in finals:
            copy.wait_recv()
        for s in range(RING - 1):
            gi_out[...] += gi_depth[s].astype(F32)

    def chunk(k):
        first, second = ("z", "y") if k % 2 == 0 else ("y", "z")
        a, b = place[first], place[second]
        start, width = starts[k], WIDTHS[k]
        size, q_start = width // RING, start // RING
        cols, q_cols = pl.ds(start, width), pl.ds(q_start, size)
        low, high = pl.ds(0, RING // 2), pl.ds(RING // 2, RING // 2)

        def block(ref, i, half=slice(None)):
            return ref.at[k, i, half] if first == "z" else ref.at[k, half, i]

        def part_of(i):
            return pl.ds(pl.multiple_of(i * quarter + q_start, 128), size)

        w_out_copies[k].wait()
        weights = w_out_v[:, q_cols, :].reshape(width, feats)
        total = nt(cot_scaled[...].reshape(2 * toks, feats), weights)
        total = total.reshape(RING, RING, -1, width)
        part[k] = total
        part16[k] = coded(total)
        yield

        up, down = at(first, 1), at(first, 3)
        across, ahead, behind = turn(a, 2), turn(a, 1), turn(a, 3)
        relays = [
            send(block(part16, across, low), relay1.at[k, 0], up),
            send(block(part16, across, high), relay1.at[k, 1], down),
        ]
        finals = []
        yield
        for n, (half, i, where) in enumerate(((low, ahead, up), (high, behind, down))):
            relays[n].wait_recv()
            mine = block(part16, i, half)
            mine[...] = coded(block(part, i, half)[...] + decoded(relay1[k, n]))
            finals.append(send(block(part16, i), final1.at[k, n], where))
        yield
        for copy in finals:
            copy.wait_recv()
        total = block(part, a)[...] + decoded(final1[k, 0]) + decoded(final1[k, 1])
        mid[k] = total
        mid16[k] = coded(total)

        finals = [
            send(mid16.at[k, turn(b, s)], final2.at[k, s - 1], at(second, s)) for s in (2, 1, 3)
        ]
        yield
        for copy in finals:
            copy.wait_recv()
        grad_act = mid[k, b]
        for n in range(RING - 1):
            grad_act += decoded(final2[k, n])
        for i in range(RING):
            slope = slope_v[:, pl.ds(i * quarter + q_start, size)]
            gp[k, i] = (grad_act[:, i * size:(i + 1) * size] * slope).astype(BF16)

        swap = [send(gp.at[k, turn(x, s)], gq.at[k, s, z, y], at("x", s)) for s in (2, 1, 3)]
        gq[k, 0, z, y] = gp[k, x]
        yield
        for copy in swap:
            copy.wait_recv()

        mine = gq.at[k, :, z, y]
        finals = [send(mine, mine, at(second, s)) for s in (2, 1, 3)]
        yield
        for copy in finals:
            copy.wait_recv()

        def rows_of(i):
            return gq.at[k, :, i] if first == "z" else gq.at[k, :, :, i]

        yield from gather(first, rows_of)

        once("acts_all", all_acts)
        total = nn(acts_all[...].reshape(feats, -1), gq[k].reshape(-1, size))
        gwi_out[:, part_of(x)] = total[:rows] * norm_factor
        finals = []
        for j in (2, 1, 3):
            xpart[k, j - 1] = total[j * rows:(j + 1) * rows].astype(BF16)
            finals.append(send(xpart.at[k, j - 1], gwi_recv.at[k, j - 1], at("x", j)))
        yield
        if (k ^ 1) in done:
            add_grad_in(k & ~1)
        done.append(k)
        yield
        settle(30)
        for copy in finals:
            copy.wait_recv()
        for j in range(1, RING):
            there = part_of(turn(x, -j))
            gwi_out[:, there] = gwi_recv[k, j - 1].astype(F32) * norm_factor

    def hidden(n):
        first, second = ("y", "z") if n % 2 == 0 else ("z", "y")
        size = PIECES[n]
        mine = pl.ds(sum(PIECES[:n]), size)

        def line(i):
            return (hid_full.at[:, i, y] if first == "z" else hid_full.at[:, z, i]).at[..., mine]

        def plane(i):
            return (hid_full.at[:, i] if second == "z" else hid_full.at[:, :, i]).at[..., mine]

        def arrived(name):
            for copy in early[name]:
                copy.wait_recv()

        once("hid_there", functools.partial(arrived, "hid"))
        yield from gather(first, line)
        yield from gather(second, plane)
        yield
        once("cot_there", functools.partial(arrived, "cot"))
        total = tn(
            hid_full[:, :, :, :, mine].reshape(-1, size), cot_full[...].reshape(-1, feats)
        )
        gwo_out[mine, :] = total * norm_factor

    work = [chunk(k) for k in range(len(WIDTHS))] + [hidden(n) for n in range(len(PIECES))] + [side(), grad_in_sum()]
    for i in ORDER:
        next(work[i], None)
    assert all(next(left, "done") == "done" for left in work)

    settle(0)
    assert len(copies.all) == n_copies, len(copies.all)


def store(*refs):
    sems = refs[-1]
    copies = []
    for src, dst in zip(refs[:3], refs[3:6]):
        rows = src.shape[0] // 4
        for n in range(4):
            piece = pl.ds(n * rows, rows)
            sem = sems.at[len(copies)]
            copies.append(pltpu.make_async_copy(src.at[piece], dst.at[piece], sem))
    for copy in copies:
        copy.start()
    for copy in copies:
        copy.wait()


def on_device(acts, cotangent, pre_act, w_in, w_out):
    hid, feats = w_out.shape
    toks, few = acts.shape[0], pre_act.shape[0]
    rows = feats // RING
    quarter = hid // RING
    quarters = (RING, RING, RING, few, quarter)
    n_copies = 22 * len(WIDTHS) + 12 * len(PIECES) + 21
    any_, vmem = pl.BlockSpec(memory_space=pl.ANY), pl.BlockSpec(memory_space=pltpu.VMEM)
    chunks, width = len(WIDTHS), WIDTHS[0]
    size, plane = width // RING, (RING, few, width)
    assert all(other == width for other in WIDTHS)
    norm_factor = 1.0 / math.sqrt(2 * toks * lax.axis_size("depth"))
    grad_in, grad_w_in, grad_w_out = pl.pallas_call(
        functools.partial(kernel, n_copies, norm_factor),
        out_shape=[
            pltpu.VMEM((toks, feats), F32),
            pltpu.VMEM((rows, hid), F32),
            pltpu.VMEM((hid // RING, feats), F32),
        ],
        in_specs=[any_] * 5,
        out_specs=[vmem] * 3,
        scratch_shapes=[
            pltpu.VMEM(quarters, BF16),
            pltpu.VMEM((toks, feats), BF16),
            pltpu.VMEM((few, hid), BF16),
            pltpu.VMEM((feats, quarter), BF16),
            pltpu.VMEM((RING, quarter, feats), BF16),
            pltpu.VMEM((2, toks, feats), BF16),
            pltpu.VMEM((2, toks, feats), BF16),
            pltpu.VMEM((RING, 2, toks, feats), BF16),
            pltpu.VMEM((chunks, RING - 1, rows, size), BF16),
            pltpu.VMEM((RING, 2, toks, feats), F32),
            pltpu.VMEM((RING, toks, feats), F32),
            pltpu.VMEM((RING - 1, toks, feats), BF16),
            pltpu.VMEM((RING - 1, toks, feats), BF16),
            pltpu.VMEM((RING, rows, 2 * toks), BF16),
            pltpu.VMEM((RING - 1, RING, rows, 2 * toks), BF16),
            pltpu.VMEM((RING, rows, RING * 2 * toks), BF16),
            pltpu.VMEM((few, hid), F32),
            pltpu.VMEM((few, hid), BF16),
            pltpu.VMEM((chunks, RING) + plane, F32),
            pltpu.VMEM((chunks, RING) + plane, BF16),
            pltpu.VMEM((chunks, 2, RING // 2) + plane[1:], BF16),
            pltpu.VMEM((chunks, 2) + plane, BF16),
            pltpu.VMEM((chunks,) + plane, F32),
            pltpu.VMEM((chunks,) + plane, BF16),
            pltpu.VMEM((chunks, RING - 1) + plane[1:], BF16),
            pltpu.VMEM((chunks, RING, few, size), BF16),
            pltpu.VMEM((chunks, RING, RING, RING, few, size), BF16),
            pltpu.VMEM((chunks, RING - 1, rows, size), BF16),
            pltpu.SemaphoreType.DMA((n_copies,)),
            pltpu.SemaphoreType.DMA((n_copies,)),
            pltpu.SemaphoreType.DMA((len(WIDTHS) + 4,)),
        ],
        compiler_params=pltpu.CompilerParams(
            collective_id=0, has_side_effects=True, vmem_limit_bytes=52 * 2**20
        ),
        cost_estimate=pl.CostEstimate(
            flops=6 * 2 * toks * feats * hid, bytes_accessed=20 * 2**20, transcendentals=few * hid
        ),
        name="backward",
    )(acts, cotangent, pre_act, w_in, w_out.reshape(RING, quarter, feats))
    outs = (grad_in, grad_w_in, grad_w_out)
    grad_in, grad_w_in, grad_w_out = pl.pallas_call(
        store,
        out_shape=[jax.ShapeDtypeStruct(out.shape, F32) for out in outs],
        in_specs=[vmem] * 3,
        out_specs=[any_] * 3,
        scratch_shapes=[pltpu.SemaphoreType.DMA((12,))],
        compiler_params=pltpu.CompilerParams(vmem_limit_bytes=4 * 2**20),
        name="store",
    )(*[pltpu.with_memory_space_constraint(out, pltpu.VMEM) for out in outs])
    return grad_in, grad_w_in[None, None], grad_w_out[None, None]


def solution(mesh):
    in_specs = (
        P(("depth", "col"), "row"),
        P(("depth", "col"), "row"),
        P(("depth", "row"), "col"),
        P("row", "col"),
        P("col", "row"),
    )
    out_specs = (
        P(("depth", "col"), "row"),
        P("row", "depth", None, "col"),
        P("col", "depth", None, "row"),
    )
    return jax.shard_map(
        on_device, mesh=mesh, in_specs=in_specs, out_specs=out_specs, check_vma=False
    )
```

```python
import functools
import math

import jax
import jax.numpy as jnp
from jax import lax
from jax.experimental import pallas as pl
from jax.experimental.pallas import tpu as pltpu
from jax.sharding import PartitionSpec as P

MESH = pl.DeviceIdType.MESH
F32, BF16 = jnp.float32, jnp.bfloat16
RING = 4
WIDTHS = (1024, 1024, 1024, 1024, 1024, 1024)
PIECES = (768, 768)
ORDER = (
    1, 1, 4, 4, 5, 0, 5, 3, 2, 2, 3, 0, 8, 8, 1, 4, 3, 0, 4, 1, 5, 3, 0, 2, 6, 4, 1, 5, 3, 7, 2, 0,
    4, 1, 3, 5, 7, 6, 2, 0, 4, 1, 5, 8, 2, 0, 1, 4, 3, 0, 5, 2, 1, 3, 4, 5, 7, 2, 0, 0, 6, 3, 1, 5,
    3, 4, 2, 2, 5, 7, 6, 4, 9, 7, 0, 3, 7, 6, 6, 9, 2, 5, 1,
)
TILE = 768

gelu_coef = 0.044715
root = math.sqrt(2.0 / math.pi)


def gelu_and_slope(v):
    tanh_u = jnp.tanh(root * (v + gelu_coef * v * v * v))
    gelu = 0.5 * v * (1.0 + tanh_u)
    slope = 0.5 * (1.0 + tanh_u) + 0.5 * v * (1.0 - tanh_u * tanh_u) * root * (
        1.0 + 3.0 * gelu_coef * v * v
    )
    return gelu, slope


def nt(left, right):
    return lax.dot_general(
        left, right, (((1,), (1,)), ((), ())), preferred_element_type=F32
    )


def nn(left, right):
    return lax.dot_general(
        left, right, (((1,), (0,)), ((), ())), preferred_element_type=F32
    )


SHIFT = 2.0**20


def coded(v):
    v = v * jnp.abs(v)
    return (v * jnp.abs(v)).astype(BF16)


def decoded(t):
    t = t.astype(F32)
    r = lax.rsqrt(jnp.maximum(jnp.abs(t), 1e-37))
    return (t * r) * (r * lax.rsqrt(r))


def tn(left, right):
    return lax.dot_general(
        left, right, (((0,), (0,)), ((), ())), preferred_element_type=F32
    )


class Copies:
    def __init__(self, send_sems, recv_sems):
        self.send_sems, self.recv_sems = send_sems, recv_sems
        self.all, self.settled = [], 0

    def send(self, src, dst, to):
        n = len(self.all)
        copy = pltpu.make_async_remote_copy(
            src_ref=src,
            dst_ref=dst,
            send_sem=self.send_sems.at[n],
            recv_sem=self.recv_sems.at[n],
            device_id=to,
            device_id_type=MESH,
        )
        copy.start()
        self.all.append(copy)
        return copy


def kernel(
    n_copies, norm_factor, acts, cot, pre, w_in, w_out,
    gi_out, gwi_out, gwo_out,
    hid_full, acts_in, pre_v, w_in_v, w_out_v, cot_v, cot_scaled, cot_full, gwi_recv, gi, gi_recv, gi_sum, gi_depth,
    acts_v, acts_x, acts_all, slope_v, hid_v,
    part, part16, relay1, final1, mid, mid16, final2, gp, gq, xpart,
    send_sems, recv_sems, local_sems,
):
    x, row, c = lax.axis_index("depth"), lax.axis_index("row"), lax.axis_index("col")
    z, y = row // RING, row % RING
    feats, hid_size = w_in.shape
    toks, rows = acts.shape[0], feats // RING
    starts = [sum(WIDTHS[:k]) for k in range(len(WIDTHS))]

    def turn(i, step):
        return lax.rem(i + (step + RING), RING)

    def at(axis, step):
        if axis == "x":
            return (turn(x, step), row, c)
        if axis == "z":
            return (x, turn(z, step) * RING + y, c)
        return (x, z * RING + turn(y, step), c)

    place = {"x": x, "y": y, "z": z}
    other_core = (x, row, 1 - c)

    quarter = hid_size // RING

    def quarter_of(i):
        return pl.ds(pl.multiple_of(i * quarter, quarter), quarter)

    w_out_copies = [
        pltpu.make_async_copy(
            w_out.at[:, pl.ds(start // RING, width // RING)],
            w_out_v.at[:, pl.ds(start // RING, width // RING)],
            local_sems.at[k],
        )
        for k, (start, width) in enumerate(zip(starts, WIDTHS))
    ]
    w_in_copy = pltpu.make_async_copy(w_in.at[:, quarter_of(x)], w_in_v, local_sems.at[len(WIDTHS)])
    cot_copy = pltpu.make_async_copy(cot, cot_v.at[c], local_sems.at[len(WIDTHS) + 1])
    acts_copy = pltpu.make_async_copy(acts, acts_in, local_sems.at[len(WIDTHS) + 2])
    pre_copy = pltpu.make_async_copy(pre, pre_v, local_sems.at[len(WIDTHS) + 3])

    partners = [other_core] + [at(axis, s) for axis in "zy" for s in (1, 2, 3)]
    partners += [(turn(x, s), row, core) for core in (c, 1 - c) for s in (1, 2, 3)]
    barrier = pltpu.get_barrier_semaphore()
    for who in partners:
        pl.semaphore_signal(barrier, inc=1, device_id=who, device_id_type=MESH)

    for copy in [cot_copy, pre_copy, *w_out_copies, acts_copy]:
        copy.start()
    lanes = pl.ds(pl.multiple_of(c * toks, toks), toks)
    cot_copy.wait()
    pl.semaphore_wait(barrier, len(partners))

    copies = Copies(send_sems, recv_sems)
    send = copies.send
    cot_core = send(cot_v.at[c], cot_v.at[c], other_core)
    w_in_copy.start()

    pre_copy.wait()

    @pl.loop(0, hid_size // TILE)
    def _(n):
        cols = pl.ds(pl.multiple_of(n * TILE, TILE), TILE)
        gelu, slope = gelu_and_slope(pre_v[:, cols].astype(F32))
        hid_v[:, cols] = gelu.astype(BF16)
        slope_v[:, cols] = slope * (1.0 / SHIFT)

    early = {}
    early["hid"] = [
        send(hid_v.at[:, quarter_of(turn(x, s))], hid_full.at[x, z, y], at("x", s))
        for s in (2, 1, 3)
    ]
    hid_full[x, z, y] = hid_v[:, quarter_of(x)]
    cot_core.wait_recv()
    cot_scaled[...] = cot_v[...] * jnp.array(SHIFT, BF16)

    def side():
        acts_copy.wait()
        turned = acts_in[...].astype(F32).T.astype(BF16)
        for j in range(RING):
            acts_v[turn(j - x, RING), :, lanes] = turned[j * rows:(j + 1) * rows]
        early["acts"] = send(acts_v.at[:, :, lanes], acts_v.at[:, :, lanes], other_core)
        yield
        early["acts_x"] = []
        for s in (1, 3, 2):
            for where in (at("x", s), (turn(x, s), row, 1 - c)):
                mine = acts_v.at[:, :, lanes]
                early["acts_x"].append(send(mine, acts_x.at[s - 1, :, :, lanes], where))
        yield
        early["cot"] = []
        for s in (1, 3, 2):
            for where in (at("x", s), (turn(x, s), row, 1 - c)):
                early["cot"].append(send(cot_v.at[c], cot_full.at[x, c], where))
        cot_full[x] = cot_v[...]

    def settle(keep):
        while len(copies.all) - copies.settled > keep:
            copies.all[copies.settled].wait_send()
            copies.settled += 1

    def gather(axis, source):
        i = place[axis]
        up, down = at(axis, 1), at(axis, 3)
        low, high = pl.ds(0, RING // 2), pl.ds(RING // 2, RING // 2)

        def push(i, depths, where):
            what = source(i).at[depths]
            return send(what, what, where)

        ups, downs = push(i, low, up), push(i, high, down)
        rest = [push(i, high, up), push(i, low, down)]
        yield
        ups.wait_recv()
        downs.wait_recv()
        rest.append(push(turn(i, 3), low, up))
        rest.append(push(turn(i, 1), high, down))
        yield
        for copy in rest:
            copy.wait_recv()

    def once(name, wait):
        if name not in early:
            early[name] = True
            wait()

    done = []

    def all_acts():
        early["acts"].wait_recv()
        for copy in early["acts_x"]:
            copy.wait_recv()
        acts_all[:, :, :2 * toks] = acts_v[...]
        for s in range(1, RING):
            there = slice(s * 2 * toks, (s + 1) * 2 * toks)
            acts_all[:RING - s, :, there] = acts_x[s - 1, s:]
            acts_all[RING - s:, :, there] = acts_x[s - 1, :s]

    def add_grad_in(k):
        once("w_in", w_in_copy.wait)
        width = (WIDTHS[k] + WIDTHS[k + 1]) // RING
        pair = jnp.concatenate([gq[k], gq[k + 1]], axis=-1).reshape(-1, width)
        total = nt(pair, w_in_v[:, pl.ds(starts[k] // RING, width)])
        total = total.reshape(gi.shape)
        early["summed"] = early.get("summed", 0) + width
        gi[...] = total if early["summed"] == width else gi[...] + total
        if early["summed"] == quarter:
            early["gi"] = send(gi.at[:, 1 - c], gi_recv, other_core)

    def grad_in_sum():
        early["gi"].wait_recv()
        gi_out[...] = gi[0, c] + gi_recv[0]
        gi_sum[...] = (gi[1:, c] + gi_recv[1:]).astype(BF16)
        finals = [send(gi_sum.at[s - 1], gi_depth.at[s - 1], at("x", -s)) for s in (2, 1, 3)]
        yield
        for copy in finals:
            copy.wait_recv()
        for s in range(RING - 1):
            gi_out[...] += gi_depth[s].astype(F32)

    def chunk(k):
        first, second = ("z", "y") if k % 2 == 0 else ("y", "z")
        a, b = place[first], place[second]
        start, width = starts[k], WIDTHS[k]
        size, q_start = width // RING, start // RING
        cols, q_cols = pl.ds(start, width), pl.ds(q_start, size)
        low, high = pl.ds(0, RING // 2), pl.ds(RING // 2, RING // 2)

        def block(ref, i, half=slice(None)):
            return ref.at[k, i, half] if first == "z" else ref.at[k, half, i]

        def part_of(i):
            return pl.ds(pl.multiple_of(i * quarter + q_start, 128), size)

        w_out_copies[k].wait()
        weights = w_out_v[:, q_cols, :].reshape(width, feats)
        total = nt(cot_scaled[...].reshape(2 * toks, feats), weights)
        total = total.reshape(RING, RING, -1, width)
        part[k] = total
        part16[k] = coded(total)
        yield

        up, down = at(first, 1), at(first, 3)
        across, ahead, behind = turn(a, 2), turn(a, 1), turn(a, 3)
        relays = [
            send(block(part16, across, low), relay1.at[k, 0], up),
            send(block(part16, across, high), relay1.at[k, 1], down),
        ]
        finals = []
        yield
        for n, (half, i, where) in enumerate(((low, ahead, up), (high, behind, down))):
            relays[n].wait_recv()
            mine = block(part16, i, half)
            mine[...] = coded(block(part, i, half)[...] + decoded(relay1[k, n]))
            finals.append(send(block(part16, i), final1.at[k, n], where))
        yield
        for copy in finals:
            copy.wait_recv()
        total = block(part, a)[...] + decoded(final1[k, 0]) + decoded(final1[k, 1])
        mid[k] = total
        mid16[k] = coded(total)

        finals = [
            send(mid16.at[k, turn(b, s)], final2.at[k, s - 1], at(second, s)) for s in (2, 1, 3)
        ]
        yield
        for copy in finals:
            copy.wait_recv()
        grad_act = mid[k, b]
        for n in range(RING - 1):
            grad_act += decoded(final2[k, n])
        for i in range(RING):
            slope = slope_v[:, pl.ds(i * quarter + q_start, size)]
            gp[k, i] = (grad_act[:, i * size:(i + 1) * size] * slope).astype(BF16)

        swap = [send(gp.at[k, turn(x, s)], gq.at[k, s, z, y], at("x", s)) for s in (2, 1, 3)]
        gq[k, 0, z, y] = gp[k, x]
        yield
        for copy in swap:
            copy.wait_recv()

        mine = gq.at[k, :, z, y]
        finals = [send(mine, mine, at(second, s)) for s in (2, 1, 3)]
        yield
        for copy in finals:
            copy.wait_recv()

        def rows_of(i):
            return gq.at[k, :, i] if first == "z" else gq.at[k, :, :, i]

        yield from gather(first, rows_of)

        once("acts_all", all_acts)
        total = nn(acts_all[...].reshape(feats, -1), gq[k].reshape(-1, size))
        gwi_out[:, part_of(x)] = total[:rows] * norm_factor
        finals = []
        for j in (2, 1, 3):
            xpart[k, j - 1] = total[j * rows:(j + 1) * rows].astype(BF16)
            finals.append(send(xpart.at[k, j - 1], gwi_recv.at[k, j - 1], at("x", j)))
        yield
        if (k ^ 1) in done:
            add_grad_in(k & ~1)
        done.append(k)
        yield
        settle(30)
        for copy in finals:
            copy.wait_recv()
        for j in range(1, RING):
            there = part_of(turn(x, -j))
            gwi_out[:, there] = gwi_recv[k, j - 1].astype(F32) * norm_factor

    def hidden(n):
        first, second = ("y", "z") if n % 2 == 0 else ("z", "y")
        size = PIECES[n]
        mine = pl.ds(sum(PIECES[:n]), size)

        def line(i):
            return (hid_full.at[:, i, y] if first == "z" else hid_full.at[:, z, i]).at[..., mine]

        def plane(i):
            return (hid_full.at[:, i] if second == "z" else hid_full.at[:, :, i]).at[..., mine]

        def arrived(name):
            for copy in early[name]:
                copy.wait_recv()

        once("hid_there", functools.partial(arrived, "hid"))
        yield from gather(first, line)
        yield from gather(second, plane)
        yield
        once("cot_there", functools.partial(arrived, "cot"))
        total = tn(
            hid_full[:, :, :, :, mine].reshape(-1, size), cot_full[...].reshape(-1, feats)
        )
        gwo_out[mine, :] = total * norm_factor

    work = [chunk(k) for k in range(len(WIDTHS))] + [hidden(n) for n in range(len(PIECES))] + [side(), grad_in_sum()]
    for n, i in enumerate(ORDER):
        if n == len(ORDER) - 3:
            settle(12)
        next(work[i], None)
    assert all(next(left, "done") == "done" for left in work)

    settle(0)
    assert len(copies.all) == n_copies, len(copies.all)


def store(*refs):
    sems = refs[-1]
    copies = [pltpu.make_async_copy(refs[i], refs[3 + i], sems.at[i]) for i in range(3)]
    for copy in copies:
        copy.start()
    for copy in copies:
        copy.wait()


def on_device(acts, cotangent, pre_act, w_in, w_out):
    hid, feats = w_out.shape
    toks, few = acts.shape[0], pre_act.shape[0]
    rows = feats // RING
    quarter = hid // RING
    quarters = (RING, RING, RING, few, quarter)
    n_copies = 22 * len(WIDTHS) + 12 * len(PIECES) + 21
    any_, vmem = pl.BlockSpec(memory_space=pl.ANY), pl.BlockSpec(memory_space=pltpu.VMEM)
    chunks, width = len(WIDTHS), WIDTHS[0]
    size, plane = width // RING, (RING, few, width)
    assert all(other == width for other in WIDTHS)
    norm_factor = 1.0 / math.sqrt(2 * toks * lax.axis_size("depth"))
    grad_in, grad_w_in, grad_w_out = pl.pallas_call(
        functools.partial(kernel, n_copies, norm_factor),
        out_shape=[
            pltpu.VMEM((toks, feats), F32),
            pltpu.VMEM((rows, hid), F32),
            pltpu.VMEM((hid // RING, feats), F32),
        ],
        in_specs=[any_] * 5,
        out_specs=[vmem] * 3,
        scratch_shapes=[
            pltpu.VMEM(quarters, BF16),
            pltpu.VMEM((toks, feats), BF16),
            pltpu.VMEM((few, hid), BF16),
            pltpu.VMEM((feats, quarter), BF16),
            pltpu.VMEM((RING, quarter, feats), BF16),
            pltpu.VMEM((2, toks, feats), BF16),
            pltpu.VMEM((2, toks, feats), BF16),
            pltpu.VMEM((RING, 2, toks, feats), BF16),
            pltpu.VMEM((chunks, RING - 1, rows, size), BF16),
            pltpu.VMEM((RING, 2, toks, feats), F32),
            pltpu.VMEM((RING, toks, feats), F32),
            pltpu.VMEM((RING - 1, toks, feats), BF16),
            pltpu.VMEM((RING - 1, toks, feats), BF16),
            pltpu.VMEM((RING, rows, 2 * toks), BF16),
            pltpu.VMEM((RING - 1, RING, rows, 2 * toks), BF16),
            pltpu.VMEM((RING, rows, RING * 2 * toks), BF16),
            pltpu.VMEM((few, hid), F32),
            pltpu.VMEM((few, hid), BF16),
            pltpu.VMEM((chunks, RING) + plane, F32),
            pltpu.VMEM((chunks, RING) + plane, BF16),
            pltpu.VMEM((chunks, 2, RING // 2) + plane[1:], BF16),
            pltpu.VMEM((chunks, 2) + plane, BF16),
            pltpu.VMEM((chunks,) + plane, F32),
            pltpu.VMEM((chunks,) + plane, BF16),
            pltpu.VMEM((chunks, RING - 1) + plane[1:], BF16),
            pltpu.VMEM((chunks, RING, few, size), BF16),
            pltpu.VMEM((chunks, RING, RING, RING, few, size), BF16),
            pltpu.VMEM((chunks, RING - 1, rows, size), BF16),
            pltpu.SemaphoreType.DMA((n_copies,)),
            pltpu.SemaphoreType.DMA((n_copies,)),
            pltpu.SemaphoreType.DMA((len(WIDTHS) + 4,)),
        ],
        compiler_params=pltpu.CompilerParams(
            collective_id=0, has_side_effects=True, vmem_limit_bytes=52 * 2**20
        ),
        cost_estimate=pl.CostEstimate(
            flops=6 * 2 * toks * feats * hid, bytes_accessed=20 * 2**20, transcendentals=few * hid
        ),
        name="backward",
    )(acts, cotangent, pre_act, w_in, w_out.reshape(RING, quarter, feats))
    outs = (grad_in, grad_w_in, grad_w_out)
    grad_in, grad_w_in, grad_w_out = pl.pallas_call(
        store,
        out_shape=[jax.ShapeDtypeStruct(out.shape, F32) for out in outs],
        in_specs=[vmem] * 3,
        out_specs=[any_] * 3,
        scratch_shapes=[pltpu.SemaphoreType.DMA((3,))],
        compiler_params=pltpu.CompilerParams(vmem_limit_bytes=4 * 2**20),
        name="store",
    )(*[pltpu.with_memory_space_constraint(out, pltpu.VMEM) for out in outs])
    return grad_in, grad_w_in[None, None], grad_w_out[None, None]


def solution(mesh):
    in_specs = (
        P(("depth", "col"), "row"),
        P(("depth", "col"), "row"),
        P(("depth", "row"), "col"),
        P("row", "col"),
        P("col", "row"),
    )
    out_specs = (
        P(("depth", "col"), "row"),
        P("row", "depth", None, "col"),
        P("col", "depth", None, "row"),
    )
    return jax.shard_map(
        on_device, mesh=mesh, in_specs=in_specs, out_specs=out_specs, check_vma=False
    )
```

```python
import functools
import math

import jax
import jax.numpy as jnp
from jax import lax
from jax.experimental import pallas as pl
from jax.experimental.pallas import tpu as pltpu
from jax.sharding import PartitionSpec as P

MESH = pl.DeviceIdType.MESH
F32, BF16 = jnp.float32, jnp.bfloat16
RING = 4
WIDTHS = (1024, 1024, 1024, 1024, 1024, 1024)
PIECES = (768, 768)
ORDER = (
    1, 1, 4, 4, 5, 0, 5, 3, 2, 2, 3, 0, 8, 8, 1, 4, 3, 0, 4, 1, 5, 3, 0, 2, 6, 4, 1, 5, 3, 7, 2, 0,
    4, 1, 3, 5, 7, 6, 2, 0, 4, 1, 5, 8, 2, 0, 1, 4, 3, 0, 5, 2, 1, 3, 4, 5, 7, 2, 0, 0, 6, 3, 1, 5,
    3, 4, 2, 2, 5, 7, 6, 4, 9, 7, 0, 3, 7, 6, 6, 9, 2, 5, 1,
)
TILE = 768

gelu_coef = 0.044715
root = math.sqrt(2.0 / math.pi)


def gelu_and_slope(v):
    tanh_u = jnp.tanh(root * (v + gelu_coef * v * v * v))
    gelu = 0.5 * v * (1.0 + tanh_u)
    slope = 0.5 * (1.0 + tanh_u) + 0.5 * v * (1.0 - tanh_u * tanh_u) * root * (
        1.0 + 3.0 * gelu_coef * v * v
    )
    return gelu, slope


def nt(left, right):
    return lax.dot_general(
        left, right, (((1,), (1,)), ((), ())), preferred_element_type=F32
    )


def nn(left, right):
    return lax.dot_general(
        left, right, (((1,), (0,)), ((), ())), preferred_element_type=F32
    )


SHIFT = 2.0**20


def coded(v):
    v = v * jnp.abs(v)
    return (v * jnp.abs(v)).astype(BF16)


def decoded(t):
    t = t.astype(F32)
    r = lax.rsqrt(jnp.maximum(jnp.abs(t), 1e-37))
    return (t * r) * (r * lax.rsqrt(r))


def tn(left, right):
    return lax.dot_general(
        left, right, (((0,), (0,)), ((), ())), preferred_element_type=F32
    )


class Copies:
    def __init__(self, send_sems, recv_sems):
        self.send_sems, self.recv_sems = send_sems, recv_sems
        self.all, self.settled = [], 0

    def send(self, src, dst, to):
        n = len(self.all)
        copy = pltpu.make_async_remote_copy(
            src_ref=src,
            dst_ref=dst,
            send_sem=self.send_sems.at[n],
            recv_sem=self.recv_sems.at[n],
            device_id=to,
            device_id_type=MESH,
        )
        copy.start()
        self.all.append(copy)
        return copy


def kernel(
    n_copies, norm_factor, acts, cot, pre, w_in, w_out,
    gi_out, gwi_out, gwo_out,
    hid_full, acts_in, pre_v, w_in_v, w_out_v, cot_v, cot_scaled, cot_full, gwi_recv, gi, gi_recv, gi_sum, gi_depth,
    acts_v, acts_x, acts_all, slope_v, hid_v,
    part, part16, relay1, final1, mid, mid16, final2, gp, gq, xpart,
    send_sems, recv_sems, local_sems,
):
    x, row, c = lax.axis_index("depth"), lax.axis_index("row"), lax.axis_index("col")
    z, y = row // RING, row % RING
    feats, hid_size = w_in.shape
    toks, rows = acts.shape[0], feats // RING
    starts = [sum(WIDTHS[:k]) for k in range(len(WIDTHS))]

    def turn(i, step):
        return lax.rem(i + (step + RING), RING)

    def at(axis, step):
        if axis == "x":
            return (turn(x, step), row, c)
        if axis == "z":
            return (x, turn(z, step) * RING + y, c)
        return (x, z * RING + turn(y, step), c)

    place = {"x": x, "y": y, "z": z}
    other_core = (x, row, 1 - c)

    quarter = hid_size // RING

    def quarter_of(i):
        return pl.ds(pl.multiple_of(i * quarter, quarter), quarter)

    w_out_copies = [
        pltpu.make_async_copy(
            w_out.at[:, pl.ds(start // RING, width // RING)],
            w_out_v.at[:, pl.ds(start // RING, width // RING)],
            local_sems.at[k],
        )
        for k, (start, width) in enumerate(zip(starts, WIDTHS))
    ]
    w_in_copy = pltpu.make_async_copy(w_in.at[:, quarter_of(x)], w_in_v, local_sems.at[len(WIDTHS)])
    cot_copy = pltpu.make_async_copy(cot, cot_v.at[c], local_sems.at[len(WIDTHS) + 1])
    acts_copy = pltpu.make_async_copy(acts, acts_in, local_sems.at[len(WIDTHS) + 2])
    pre_copy = pltpu.make_async_copy(pre, pre_v, local_sems.at[len(WIDTHS) + 3])

    partners = [other_core] + [at(axis, s) for axis in "zy" for s in (1, 2, 3)]
    partners += [at("x", s) for s in (1, 2, 3)]
    barrier = pltpu.get_barrier_semaphore()
    for who in partners:
        pl.semaphore_signal(barrier, inc=1, device_id=who, device_id_type=MESH)

    for copy in [cot_copy, pre_copy, *w_out_copies, acts_copy]:
        copy.start()
    lanes = pl.ds(pl.multiple_of(c * toks, toks), toks)
    cot_copy.wait()
    pl.semaphore_wait(barrier, len(partners))

    copies = Copies(send_sems, recv_sems)
    send = copies.send
    cot_core = send(cot_v.at[c], cot_v.at[c], other_core)
    w_in_copy.start()

    pre_copy.wait()

    @pl.loop(0, hid_size // TILE)
    def _(n):
        cols = pl.ds(pl.multiple_of(n * TILE, TILE), TILE)
        gelu, slope = gelu_and_slope(pre_v[:, cols].astype(F32))
        hid_v[:, cols] = gelu.astype(BF16)
        slope_v[:, cols] = slope * (1.0 / SHIFT)

    early = {}
    early["hid"] = [
        send(hid_v.at[:, quarter_of(turn(x, s))], hid_full.at[x, z, y], at("x", s))
        for s in (2, 1, 3)
    ]
    hid_full[x, z, y] = hid_v[:, quarter_of(x)]
    cot_core.wait_recv()
    cot_scaled[...] = cot_v[...] * jnp.array(SHIFT, BF16)

    def side():
        acts_copy.wait()
        turned = acts_in[...].astype(F32).T.astype(BF16)
        for j in range(RING):
            acts_v[turn(j - x, RING), :, lanes] = turned[j * rows:(j + 1) * rows]
        early["acts"] = send(acts_v.at[:, :, lanes], acts_v.at[:, :, lanes], other_core)
        yield
        mine = acts_v.at[:, :, lanes]
        early["acts_x"] = [send(mine, acts_x.at[s - 1, :, :, lanes], at("x", s)) for s in (1, 3, 2)]
        early["cot"] = [send(cot_v.at[c], cot_full.at[x, c], at("x", s)) for s in (1, 3, 2)]
        yield
        for copy, s in zip(list(early["acts_x"]), (1, 3, 2)):
            copy.wait_recv()
            here = acts_x.at[s - 1, :, :, lanes]
            early["acts_x"].append(send(here, here, other_core))
        for copy, s in zip(list(early["cot"]), (1, 3, 2)):
            copy.wait_recv()
            here = cot_full.at[turn(x, -s), c]
            early["cot"].append(send(here, here, other_core))
        del early["acts_x"][:3], early["cot"][:3]
        cot_full[x] = cot_v[...]

    def settle(keep):
        while len(copies.all) - copies.settled > keep:
            copies.all[copies.settled].wait_send()
            copies.settled += 1

    def gather(axis, source):
        i = place[axis]
        up, down = at(axis, 1), at(axis, 3)
        low, high = pl.ds(0, RING // 2), pl.ds(RING // 2, RING // 2)

        def push(i, depths, where):
            what = source(i).at[depths]
            return send(what, what, where)

        ups, downs = push(i, low, up), push(i, high, down)
        rest = [push(i, high, up), push(i, low, down)]
        yield
        ups.wait_recv()
        downs.wait_recv()
        rest.append(push(turn(i, 3), low, up))
        rest.append(push(turn(i, 1), high, down))
        yield
        for copy in rest:
            copy.wait_recv()

    def once(name, wait):
        if name not in early:
            early[name] = True
            wait()

    done = []

    def all_acts():
        early["acts"].wait_recv()
        for copy in early["acts_x"]:
            copy.wait_recv()
        acts_all[:, :, :2 * toks] = acts_v[...]
        for s in range(1, RING):
            there = slice(s * 2 * toks, (s + 1) * 2 * toks)
            acts_all[:RING - s, :, there] = acts_x[s - 1, s:]
            acts_all[RING - s:, :, there] = acts_x[s - 1, :s]

    def add_grad_in(k):
        once("w_in", w_in_copy.wait)
        width = (WIDTHS[k] + WIDTHS[k + 1]) // RING
        pair = jnp.concatenate([gq[k], gq[k + 1]], axis=-1).reshape(-1, width)
        total = nt(pair, w_in_v[:, pl.ds(starts[k] // RING, width)])
        total = total.reshape(gi.shape)
        early["summed"] = early.get("summed", 0) + width
        gi[...] = total if early["summed"] == width else gi[...] + total
        if early["summed"] == quarter:
            early["gi"] = send(gi.at[:, 1 - c], gi_recv, other_core)

    def grad_in_sum():
        early["gi"].wait_recv()
        gi_out[...] = gi[0, c] + gi_recv[0]
        gi_sum[...] = (gi[1:, c] + gi_recv[1:]).astype(BF16)
        finals = [send(gi_sum.at[s - 1], gi_depth.at[s - 1], at("x", -s)) for s in (2, 1, 3)]
        yield
        for copy in finals:
            copy.wait_recv()
        for s in range(RING - 1):
            gi_out[...] += gi_depth[s].astype(F32)

    def chunk(k):
        first, second = ("z", "y") if k % 2 == 0 else ("y", "z")
        a, b = place[first], place[second]
        start, width = starts[k], WIDTHS[k]
        size, q_start = width // RING, start // RING
        cols, q_cols = pl.ds(start, width), pl.ds(q_start, size)
        low, high = pl.ds(0, RING // 2), pl.ds(RING // 2, RING // 2)

        def block(ref, i, half=slice(None)):
            return ref.at[k, i, half] if first == "z" else ref.at[k, half, i]

        def part_of(i):
            return pl.ds(pl.multiple_of(i * quarter + q_start, 128), size)

        w_out_copies[k].wait()
        weights = w_out_v[:, q_cols, :].reshape(width, feats)
        total = nt(cot_scaled[...].reshape(2 * toks, feats), weights)
        total = total.reshape(RING, RING, -1, width)
        part[k] = total
        part16[k] = coded(total)
        yield

        up, down = at(first, 1), at(first, 3)
        across, ahead, behind = turn(a, 2), turn(a, 1), turn(a, 3)
        relays = [
            send(block(part16, across, low), relay1.at[k, 0], up),
            send(block(part16, across, high), relay1.at[k, 1], down),
        ]
        finals = []
        yield
        for n, (half, i, where) in enumerate(((low, ahead, up), (high, behind, down))):
            relays[n].wait_recv()
            mine = block(part16, i, half)
            mine[...] = coded(block(part, i, half)[...] + decoded(relay1[k, n]))
            finals.append(send(block(part16, i), final1.at[k, n], where))
        yield
        for copy in finals:
            copy.wait_recv()
        total = block(part, a)[...] + decoded(final1[k, 0]) + decoded(final1[k, 1])
        mid[k] = total
        mid16[k] = coded(total)

        finals = [
            send(mid16.at[k, turn(b, s)], final2.at[k, s - 1], at(second, s)) for s in (2, 1, 3)
        ]
        yield
        for copy in finals:
            copy.wait_recv()
        grad_act = mid[k, b]
        for n in range(RING - 1):
            grad_act += decoded(final2[k, n])
        for i in range(RING):
            slope = slope_v[:, pl.ds(i * quarter + q_start, size)]
            gp[k, i] = (grad_act[:, i * size:(i + 1) * size] * slope).astype(BF16)

        swap = [send(gp.at[k, turn(x, s)], gq.at[k, s, z, y], at("x", s)) for s in (2, 1, 3)]
        gq[k, 0, z, y] = gp[k, x]
        yield
        for copy in swap:
            copy.wait_recv()

        mine = gq.at[k, :, z, y]
        finals = [send(mine, mine, at(second, s)) for s in (2, 1, 3)]
        yield
        for copy in finals:
            copy.wait_recv()

        def rows_of(i):
            return gq.at[k, :, i] if first == "z" else gq.at[k, :, :, i]

        yield from gather(first, rows_of)

        once("acts_all", all_acts)
        total = nn(acts_all[...].reshape(feats, -1), gq[k].reshape(-1, size))
        gwi_out[:, part_of(x)] = total[:rows] * norm_factor
        finals = []
        for j in (2, 1, 3):
            xpart[k, j - 1] = total[j * rows:(j + 1) * rows].astype(BF16)
            finals.append(send(xpart.at[k, j - 1], gwi_recv.at[k, j - 1], at("x", j)))
        yield
        if (k ^ 1) in done:
            add_grad_in(k & ~1)
        done.append(k)
        yield
        settle(30)
        for copy in finals:
            copy.wait_recv()
        for j in range(1, RING):
            there = part_of(turn(x, -j))
            gwi_out[:, there] = gwi_recv[k, j - 1].astype(F32) * norm_factor

    def hidden(n):
        first, second = ("y", "z") if n % 2 == 0 else ("z", "y")
        size = PIECES[n]
        mine = pl.ds(sum(PIECES[:n]), size)

        def line(i):
            return (hid_full.at[:, i, y] if first == "z" else hid_full.at[:, z, i]).at[..., mine]

        def plane(i):
            return (hid_full.at[:, i] if second == "z" else hid_full.at[:, :, i]).at[..., mine]

        def arrived(name):
            for copy in early[name]:
                copy.wait_recv()

        once("hid_there", functools.partial(arrived, "hid"))
        yield from gather(first, line)
        yield from gather(second, plane)
        yield
        once("cot_there", functools.partial(arrived, "cot"))
        total = tn(
            hid_full[:, :, :, :, mine].reshape(-1, size), cot_full[...].reshape(-1, feats)
        )
        gwo_out[mine, :] = total * norm_factor

    work = [chunk(k) for k in range(len(WIDTHS))] + [hidden(n) for n in range(len(PIECES))] + [side(), grad_in_sum()]
    for n, i in enumerate(ORDER):
        if n == len(ORDER) - 3:
            settle(12)
        next(work[i], None)
    assert all(next(left, "done") == "done" for left in work)

    settle(0)
    assert len(copies.all) == n_copies, len(copies.all)


def store(*refs):
    sems = refs[-1]
    copies = [pltpu.make_async_copy(refs[i], refs[3 + i], sems.at[i]) for i in range(3)]
    for copy in copies:
        copy.start()
    for copy in copies:
        copy.wait()


def on_device(acts, cotangent, pre_act, w_in, w_out):
    hid, feats = w_out.shape
    toks, few = acts.shape[0], pre_act.shape[0]
    rows = feats // RING
    quarter = hid // RING
    quarters = (RING, RING, RING, few, quarter)
    n_copies = 22 * len(WIDTHS) + 12 * len(PIECES) + 21
    any_, vmem = pl.BlockSpec(memory_space=pl.ANY), pl.BlockSpec(memory_space=pltpu.VMEM)
    chunks, width = len(WIDTHS), WIDTHS[0]
    size, plane = width // RING, (RING, few, width)
    assert all(other == width for other in WIDTHS)
    norm_factor = 1.0 / math.sqrt(2 * toks * lax.axis_size("depth"))
    grad_in, grad_w_in, grad_w_out = pl.pallas_call(
        functools.partial(kernel, n_copies, norm_factor),
        out_shape=[
            pltpu.VMEM((toks, feats), F32),
            pltpu.VMEM((rows, hid), F32),
            pltpu.VMEM((hid // RING, feats), F32),
        ],
        in_specs=[any_] * 5,
        out_specs=[vmem] * 3,
        scratch_shapes=[
            pltpu.VMEM(quarters, BF16),
            pltpu.VMEM((toks, feats), BF16),
            pltpu.VMEM((few, hid), BF16),
            pltpu.VMEM((feats, quarter), BF16),
            pltpu.VMEM((RING, quarter, feats), BF16),
            pltpu.VMEM((2, toks, feats), BF16),
            pltpu.VMEM((2, toks, feats), BF16),
            pltpu.VMEM((RING, 2, toks, feats), BF16),
            pltpu.VMEM((chunks, RING - 1, rows, size), BF16),
            pltpu.VMEM((RING, 2, toks, feats), F32),
            pltpu.VMEM((RING, toks, feats), F32),
            pltpu.VMEM((RING - 1, toks, feats), BF16),
            pltpu.VMEM((RING - 1, toks, feats), BF16),
            pltpu.VMEM((RING, rows, 2 * toks), BF16),
            pltpu.VMEM((RING - 1, RING, rows, 2 * toks), BF16),
            pltpu.VMEM((RING, rows, RING * 2 * toks), BF16),
            pltpu.VMEM((few, hid), F32),
            pltpu.VMEM((few, hid), BF16),
            pltpu.VMEM((chunks, RING) + plane, F32),
            pltpu.VMEM((chunks, RING) + plane, BF16),
            pltpu.VMEM((chunks, 2, RING // 2) + plane[1:], BF16),
            pltpu.VMEM((chunks, 2) + plane, BF16),
            pltpu.VMEM((chunks,) + plane, F32),
            pltpu.VMEM((chunks,) + plane, BF16),
            pltpu.VMEM((chunks, RING - 1) + plane[1:], BF16),
            pltpu.VMEM((chunks, RING, few, size), BF16),
            pltpu.VMEM((chunks, RING, RING, RING, few, size), BF16),
            pltpu.VMEM((chunks, RING - 1, rows, size), BF16),
            pltpu.SemaphoreType.DMA((n_copies,)),
            pltpu.SemaphoreType.DMA((n_copies,)),
            pltpu.SemaphoreType.DMA((len(WIDTHS) + 4,)),
        ],
        compiler_params=pltpu.CompilerParams(
            collective_id=0, has_side_effects=True, vmem_limit_bytes=52 * 2**20
        ),
        cost_estimate=pl.CostEstimate(
            flops=6 * 2 * toks * feats * hid, bytes_accessed=20 * 2**20, transcendentals=few * hid
        ),
        name="backward",
    )(acts, cotangent, pre_act, w_in, w_out.reshape(RING, quarter, feats))
    outs = (grad_in, grad_w_in, grad_w_out)
    grad_in, grad_w_in, grad_w_out = pl.pallas_call(
        store,
        out_shape=[jax.ShapeDtypeStruct(out.shape, F32) for out in outs],
        in_specs=[vmem] * 3,
        out_specs=[any_] * 3,
        scratch_shapes=[pltpu.SemaphoreType.DMA((3,))],
        compiler_params=pltpu.CompilerParams(vmem_limit_bytes=4 * 2**20),
        name="store",
    )(*[pltpu.with_memory_space_constraint(out, pltpu.VMEM) for out in outs])
    return grad_in, grad_w_in[None, None], grad_w_out[None, None]


def solution(mesh):
    in_specs = (
        P(("depth", "col"), "row"),
        P(("depth", "col"), "row"),
        P(("depth", "row"), "col"),
        P("row", "col"),
        P("col", "row"),
    )
    out_specs = (
        P(("depth", "col"), "row"),
        P("row", "depth", None, "col"),
        P("col", "depth", None, "row"),
    )
    return jax.shard_map(
        on_device, mesh=mesh, in_specs=in_specs, out_specs=out_specs, check_vma=False
    )
```
